128 devices in a mesh: seq: 16 (over z, x), table: 8 (over y, core).
Axes of the slice: x: 4, y: 4, z: 4, core: 2. Of those that a mesh axis runs over, the one named last changes fastest.
Arguments:
- hidden: bfloat16 [65536, 768], P(('seq', 'table')), may hold values from -6 to 6
- gain: float32 [768], replicated, may hold values from 0.5 to 1.5
- queries: bfloat16 [65536, 768], P(('seq', 'table')), may hold values from -40 to 40
- keys: bfloat16 [65536, 768], P(('seq', 'table')), may hold values from -40 to 40
- values: bfloat16 [65536, 768], P(('seq', 'table')), may hold values from -6 to 6
- w_query: bfloat16 [768, 768], replicated, may hold values from -0.21875 to 0.21875
- w_key: bfloat16 [768, 768], replicated, may hold values from -0.21875 to 0.21875
- w_value: bfloat16 [768, 768], replicated, may hold values from -0.21875 to 0.21875
- w_out: bfloat16 [768, 768], replicated, may hold values from -0.21875 to 0.21875
- grad_out: bfloat16 [65536, 768], P(('seq', 'table')), may hold values from -6 to 6
- doc_lengths: int32 [64], replicated, may hold values from 1 to 4096, 65536 in all
- hash_ids: int32 [2, 65536], P(None, ('seq', 'table')), may hold values from 0 to 262143, as said below
Outputs:
- grad_hidden: bfloat16 [65536, 768], P(('seq', 'table'))
- table_grads: bfloat16 [2, 262144, 768], P(None, ('seq', 'table'))
The draws below stay inside these ranges and needn't reach their ends.
Inputs may be any that keep to these rules, and one draw needn't show every extreme that they name: `hash_ids`: rows owner * 2048 to owner * 2048 + 2047 belong to device owner of seq+table. Among the 512 bytes of one device, at most 20 have their row of one table at one owner, and these name at most 5 distinct rows; in every table each device sends exactly 20 bytes naming exactly 5 distinct rows to some owner.
All inputs are finite; a program needn't handle non-finite values.
Results may differ from the reference program's by a relative error of at most 0.0094.
Values may be sent and summed in bfloat16 or wider, within the bound.
No kernel may reach another device: no remote copies, remote signals or barrier semaphores. Data moves between devices by JAX's collectives and lax.ppermute only.
A program may use at most 192 MiB of HBM per device.

```python
import math
import jax
import jax.numpy as jnp
import numpy as np
from jax import lax

D = 768
HEADS = 12
HD = 64
TOK_DEV = 512
WINDOW = 512
NG = 2
ROWS_DEV = 2048
HOT = 16
DOC_MEAN = 1024
TOKENS = 65536
ROWS = 262144
DOCS = 64


def draw_queries(key, part):
    key = jax.random.fold_in(key, 11)
    drawn = jnp.clip(jax.random.normal(key, (TOKENS, D), jnp.float32), -6.0, 6.0)
    return drawn.astype(jnp.bfloat16)


def draw_keys(key, part):
    key = jax.random.fold_in(key, 23)
    drawn = jnp.clip(jax.random.normal(key, (TOKENS, D), jnp.float32), -6.0, 6.0)
    return drawn.astype(jnp.bfloat16)


def draw_hash_ids(key, part):
    key = jax.random.fold_in(key, 37)
    blocks = TOKENS // TOK_DEV
    spread_count = TOK_DEV - HOT
    most = (spread_count + blocks - 1) // blocks
    many = jax.random.split(key, NG * blocks)

    def one_block(block_key):
        pick, rows_key, common_key, order_key = jax.random.split(block_key, 4)
        offset = jax.random.randint(pick, (), 0, blocks, jnp.int32)
        index = jnp.arange(spread_count, dtype=jnp.int32)
        spread = (index + offset) % blocks
        owners = jnp.concatenate([jnp.full((HOT,), offset, jnp.int32), spread])
        common = jax.random.randint(common_key, (), 0, ROWS_DEV, jnp.int32)
        jumps = jax.random.randint(rows_key, (spread_count,), 0, (ROWS_DEV - 1) // most, jnp.int32)
        spread_rows = (common + 1 + index // blocks + most * jumps) % ROWS_DEV
        local = jnp.concatenate([jnp.full((HOT,), common, jnp.int32), spread_rows])
        return jax.random.permutation(order_key, owners * ROWS_DEV + local)
    return jax.vmap(one_block)(many).reshape(NG, TOKENS).astype(jnp.int32)


def level_of(stream_key, dims, shards, smallest, high):
    level = 1.0
    for axis_at, parts in shards:
        heights = jax.random.uniform(jax.random.fold_in(jax.random.fold_in(stream_key, 6), axis_at), (parts,), jnp.float32, smallest / len(shards), high / len(shards))
        level = level * jnp.repeat(jnp.exp(heights), dims[axis_at] // parts).reshape((-1,) + (1,) * (len(dims) - 1 - axis_at))
    return level


def length_profile(amount, total, limit, skew):
    portions = [(1 << 20) // math.isqrt(grade ** skew) + 1 for grade in range(2, amount + 1)]
    rest, counts = total - limit - (amount - 1), [1] * (amount - 1)
    while rest > 0:
        candidates = [i for i in range(amount - 1) if counts[i] < limit]
        whole, left = sum([portions[i] for i in candidates]), rest
        for i in candidates:
            extra = min(limit - counts[i], max(1, left * portions[i] // whole), rest)
            counts[i] = counts[i] + extra
            rest = rest - extra
    return np.array([limit] + counts)


def uneven_parts(rng, amount, total, most, lean):
    if amount == 2:
        one = jax.random.randint(rng, (), max(1, total - most), min(most, total - 1) + 1)
        return jnp.stack([one, total - one])
    lengths = jnp.asarray(length_profile(amount, total, most, lean), jnp.int32)
    twos = (amount - 1) // 2
    source_of, taker = lengths[1:1 + 2 * twos:2], lengths[2:2 + 2 * twos:2]
    slack = jnp.minimum(source_of - 1, most - taker)
    moved = jax.random.randint(jax.random.fold_in(rng, 1), (twos,), 0, 1 << 20) % (slack + 1)
    lengths = lengths.at[1:1 + 2 * twos:2].set(source_of - moved).at[2:2 + 2 * twos:2].set(taker + moved)
    return lengths[jax.random.permutation(jax.random.fold_in(rng, 2), amount)]


def noise(rng, dims, scale, limit, cuts=(), held_as=jnp.bfloat16):
    result = jax.random.normal(rng, dims, jnp.float32) * scale
    if len(cuts) > 0:
        result = level_of(rng, dims, cuts, -0.22, 0.18) * result
    return jnp.clip(result, min=-limit, max=limit).astype(held_as)


def setup_inputs(seed: int = 0) -> dict:
    streams_of = jax.random.split(jax.random.key(seed), 13)
    hidden = noise(streams_of[0], (TOKENS, D), 1.0, 6.0, ((0, 128),))
    gain = jnp.clip(1.0 + 0.1 * jax.random.normal(streams_of[1], (D,), jnp.float32), 0.5, 1.5)
    queries = draw_queries(jax.random.fold_in(streams_of[12], 71), 0)
    keys = draw_keys(jax.random.fold_in(streams_of[12], 71), 0)
    values = noise(streams_of[4], (TOKENS, D), 1.0, 6.0, ((0, 128),))
    w_query = noise(streams_of[5], (D, D), D ** -0.5, 0.21875)
    w_key = noise(streams_of[6], (D, D), D ** -0.5, 0.21875)
    w_value = noise(streams_of[7], (D, D), D ** -0.5, 0.21875)
    w_out = noise(streams_of[8], (D, D), D ** -0.5, 0.21875)
    grad_out = noise(streams_of[9], (TOKENS, D), 1.0, 6.0, ((0, 128),))
    doc_lengths = uneven_parts(streams_of[10], DOCS, TOKENS, 4 * DOC_MEAN, 2).astype(jnp.int32)
    hash_ids = draw_hash_ids(jax.random.fold_in(streams_of[12], 71), 0)
    return {"hidden": hidden, "gain": gain, "queries": queries, "keys": keys, "values": values, "w_query": w_query, "w_key": w_key, "w_value": w_value, "w_out": w_out, "grad_out": grad_out, "doc_lengths": doc_lengths, "hash_ids": hash_ids}


EPS = 1e-06
NEG = -1e+30

def times_transpose(left, weight):
    return lax.dot_general(left, weight, (((1,), (1,)), ((), ())), preferred_element_type=jnp.float32)

def doc_index(positions, ends):
    return lax.optimization_barrier(jnp.sum((positions[:, None] >= ends[None, :]).astype(jnp.int32), axis=1))

def allowed(qpos, kpos, ends):
    diff = qpos[:, None] - kpos[None, :]
    same = doc_index(qpos, ends)[:, None] == doc_index(kpos, ends)[None, :]
    return (diff >= 0) & (diff < WINDOW) & (kpos[None, :] >= 0) & same

def tile_grads(qb, kb, vb, dab, mask):
    scale = HD ** (-0.5)
    rows = qb.shape[0]
    cols = kb.shape[0]
    q = qb.reshape(rows, HEADS, HD).astype(jnp.float32)
    k = kb.reshape(cols, HEADS, HD).astype(jnp.float32)
    v = vb.reshape(cols, HEADS, HD).astype(jnp.float32)
    da = dab.reshape(rows, HEADS, HD).astype(jnp.float32)
    score = jnp.einsum('qhd,khd->hqk', q, k) * scale
    score = jnp.where(mask[None], score, NEG)
    top = lax.optimization_barrier(jnp.max(score, axis=2, keepdims=True))
    expo = jnp.where(mask[None], jnp.exp(score - top), 0.0)
    total = lax.optimization_barrier(jnp.sum(expo, axis=2, keepdims=True))
    prob = expo / total
    lowprob = prob.astype(jnp.bfloat16).astype(jnp.float32)
    attn = jnp.einsum('hqk,khd->qhd', lowprob, v)
    delta = lax.optimization_barrier(jnp.sum(attn * da, axis=2))
    dprob = jnp.einsum('qhd,khd->hqk', da, v)
    dscore = (prob * (dprob - jnp.transpose(delta)[:, :, None]) * scale).astype(jnp.bfloat16).astype(jnp.float32)
    grad_q = jnp.einsum('hqk,khd->qhd', dscore, k)
    grad_k = jnp.einsum('hqk,qhd->khd', dscore, q)
    grad_v = jnp.einsum('hqk,qhd->khd', lowprob, da)
    return (grad_q.reshape(rows, -1), grad_k.reshape(cols, -1), grad_v.reshape(cols, -1))

def reference(hidden, gain, queries, keys, values, w_query, w_key, w_value, w_out, grad_out, doc_lengths, hash_ids):
    grad_attn = times_transpose(grad_out, w_out).astype(jnp.bfloat16)
    ends = jnp.cumsum(doc_lengths).astype(jnp.int32)
    front = jnp.zeros((WINDOW, D), jnp.bfloat16)
    keys_pad = jnp.concatenate([front, keys], axis=0)
    values_pad = jnp.concatenate([front, values], axis=0)
    block = min(512, TOK_DEV)
    number = TOKENS // block

    def step(carry, index):
        dk_acc, dv_acc = carry
        start = (index * block).astype(jnp.int32)
        qb = lax.dynamic_slice_in_dim(queries, start, block, 0)
        dab = lax.dynamic_slice_in_dim(grad_attn, start, block, 0)
        kb = lax.dynamic_slice_in_dim(keys_pad, start, block + WINDOW, 0)
        vb = lax.dynamic_slice_in_dim(values_pad, start, block + WINDOW, 0)
        qpos = start + jnp.arange(block, dtype=jnp.int32)
        kpos = start - WINDOW + jnp.arange(block + WINDOW, dtype=jnp.int32)
        grad_q, grad_k, grad_v = tile_grads(qb, kb, vb, dab, allowed(qpos, kpos, ends))
        dk_acc = lax.dynamic_update_slice_in_dim(dk_acc, lax.dynamic_slice_in_dim(dk_acc, start, block + WINDOW, 0) + grad_k, start, 0)
        dv_acc = lax.dynamic_update_slice_in_dim(dv_acc, lax.dynamic_slice_in_dim(dv_acc, start, block + WINDOW, 0) + grad_v, start, 0)
        return ((dk_acc, dv_acc), grad_q.astype(jnp.bfloat16))
    zero = jnp.zeros((TOKENS + WINDOW, D), jnp.float32)
    (dk_acc, dv_acc), dq_blocks = lax.scan(step, (zero, zero), jnp.arange(number, dtype=jnp.int32))
    grad_q = dq_blocks.reshape(TOKENS, D)
    grad_k = dk_acc[WINDOW:].astype(jnp.bfloat16)
    grad_v = dv_acc[WINDOW:].astype(jnp.bfloat16)
    grad_norm = times_transpose(grad_q, w_query) + times_transpose(grad_k, w_key) + times_transpose(grad_v, w_value)
    full = hidden.astype(jnp.float32)
    inverse = lax.rsqrt(lax.optimization_barrier(jnp.mean(full * full, axis=1, keepdims=True)) + EPS)
    unit = full * inverse
    scaled = grad_norm * gain[None, :]
    through = inverse * (scaled - unit * lax.optimization_barrier(jnp.mean(scaled * unit, axis=1, keepdims=True)))
    grad_hidden = (grad_out.astype(jnp.float32) + through).astype(jnp.bfloat16)
    wide = grad_hidden.astype(jnp.float32)
    tables = jnp.stack([jax.ops.segment_sum(wide, hash_ids[table], num_segments=ROWS) for table in range(NG)])
    return (grad_hidden, tables.astype(jnp.bfloat16))
```

```python
import functools

import jax
import jax.numpy as jnp
from jax import lax
from jax.experimental import pallas as pl
from jax.experimental.pallas import tpu as pltpu
from jax.sharding import PartitionSpec as P

HD = 64
WINDOW = 512
NG = 2
ROWS_DEV = 2048
SLOTS = 5
EPS = 1e-06
NEG = -1e30
AXES = ("seq", "table")
LANES = 128
BF16 = jnp.bfloat16
F32 = jnp.float32
I32 = jnp.int32
VMEM_BYTES = 56 * 1024 * 1024


def iota(shape, dim):
    return lax.broadcasted_iota(I32, shape, dim)


def dot(left, right, left_dim, right_dim):
    return lax.dot_general(
        left, right, (((left_dim,), (right_dim,)), ((), ())), preferred_element_type=F32
    )


def params():
    return pltpu.CompilerParams(vmem_limit_bytes=VMEM_BYTES)


def shifted(shard, by):
    count = lax.axis_size(AXES)
    pairs = [(i, i + by) for i in range(count) if 0 <= i + by < count]
    return lax.ppermute(shard, AXES, pairs)


def slots_kernel(row_ref, col_ref, slot_ref, label_ref):
    count = row_ref.shape[1]
    places = label_ref.shape[1]
    labels = jnp.full((1, places), ROWS_DEV, I32)
    sub = iota((count, count), 0)
    lane = iota((count, count), 1)
    for table in range(NG):
        row = row_ref[table : table + 1, :]
        col = col_ref[:, table : table + 1]
        same = col == row
        first_col = jnp.sum((same & (lane < sub)).astype(I32), axis=1, keepdims=True) == 0
        first_row = jnp.sum((same & (sub < lane)).astype(I32), axis=0, keepdims=True) == 0
        row_owner = row // ROWS_DEV
        col_owner = col // ROWS_DEV
        mates = row_owner == col_owner
        place_row = jnp.sum((first_col & mates & (col < row)).astype(I32), axis=0, keepdims=True)
        place_col = jnp.sum((first_row & mates & (row < col)).astype(I32), axis=1, keepdims=True)
        base = table * SLOTS
        slot_ref[table : table + 1, :] = row_owner * (NG * SLOTS) + base + place_row
        slot_col = col_owner * (NG * SLOTS) + base + place_col
        local_col = col - col_owner * ROWS_DEV
        hit = slot_col == iota((count, places), 1)
        labels = jnp.minimum(
            labels, jnp.min(jnp.where(hit, local_col, ROWS_DEV), axis=0, keepdims=True)
        )
    label_ref[...] = labels


def make_slots(hash_ids, devices):
    count = hash_ids.shape[1]
    places = devices * NG * SLOTS
    return pl.pallas_call(
        slots_kernel,
        out_shape=(
            jax.ShapeDtypeStruct((NG, count), I32),
            jax.ShapeDtypeStruct((1, places), I32),
        ),
        compiler_params=params(),
        name="slots",
    )(hash_ids, jnp.transpose(hash_ids))


QT = 256
KT = QT + WINDOW


def attention_kernel(
    first_ref, len_ref, q_ref, kp_ref, ko_ref, vp_ref, vo_ref, da_ref,
    dq_ref, dkp_ref, dvp_ref, dko_ref, dvo_ref,
    bias_ref, kx_ref, vx_ref, dk_ref, dv_ref,
):
    count = q_ref.shape[0]
    tiles = count // QT

    @pl.when(pl.program_id(0) == 0)
    def _():
        docs = len_ref.shape[1]
        first = first_ref[0]
        upto = iota((docs, docs), 1) <= iota((docs, docs), 0)
        ends = jnp.sum(jnp.where(upto, len_ref[...], 0), axis=1, keepdims=True)
        qpos = first + iota((1, count), 1)
        start = jnp.max(jnp.where(ends <= qpos, ends, 0), axis=0, keepdims=True)
        low = jnp.maximum(start, qpos - (WINDOW - 1))
        for tile in range(tiles):
            cols = slice(tile * QT, (tile + 1) * QT)
            kpos = first - WINDOW + tile * QT + iota((KT, QT), 0)
            ok = (kpos >= low[:, cols]) & (kpos <= qpos[:, cols])
            bias_ref[tile] = jnp.where(ok, 0.0, NEG)

    kx_ref[:WINDOW] = kp_ref[...]
    kx_ref[WINDOW:] = ko_ref[...]
    vx_ref[:WINDOW] = vp_ref[...]
    vx_ref[WINDOW:] = vo_ref[...]
    lane = iota((QT, LANES), 1)
    scale = HD ** (-0.5)
    zero = jnp.zeros((QT, LANES), BF16)
    for tile in range(tiles):
        rows = slice(tile * QT, (tile + 1) * QT)
        span = slice(tile * QT, tile * QT + KT)
        q = q_ref[rows, :] * jnp.asarray(scale, BF16)
        da = da_ref[rows, :]
        k = kx_ref[span, :]
        v = vx_ref[span, :]
        dq = dk = dv = None
        for half in range(LANES // HD):
            mine = (lane // HD) == half
            qh = jnp.where(mine, q, zero)
            dah = jnp.where(mine, da, zero)
            score = dot(k, qh, 1, 1) + bias_ref[tile]
            top = jnp.max(score, axis=0, keepdims=True)
            expo = jnp.exp(score - top)
            total = jnp.sum(expo, axis=0, keepdims=True)
            prob = expo * (1.0 / total)
            lowprob = prob.astype(BF16)
            dprob = dot(v, dah, 1, 1)
            delta = jnp.sum(lowprob.astype(F32) * dprob, axis=0, keepdims=True)
            dscore = (prob * (dprob - delta)).astype(BF16)
            dvh = dot(lowprob, dah, 1, 0)
            dkh = dot(dscore, qh, 1, 0)
            dqh = jnp.where(mine, dot(dscore, k, 0, 0), 0.0)
            dv = dvh if dv is None else dv + dvh
            dk = dkh if dk is None else dk + dkh
            dq = dqh if dq is None else dq + dqh
        dq_ref[rows, :] = (dq * scale).astype(BF16)
        if tile == 0:
            dk_ref[span, :] = dk
            dv_ref[span, :] = dv
        else:
            seen = slice(tile * QT, (tile - 1) * QT + KT)
            fresh = slice((tile - 1) * QT + KT, tile * QT + KT)
            both = KT - QT
            dk_ref[seen, :] += dk[:both]
            dv_ref[seen, :] += dv[:both]
            dk_ref[fresh, :] = dk[both:]
            dv_ref[fresh, :] = dv[both:]
    dkp_ref[...] = dk_ref[:WINDOW].astype(BF16)
    dvp_ref[...] = dv_ref[:WINDOW].astype(BF16)
    dko_ref[...] = dk_ref[WINDOW:]
    dvo_ref[...] = dv_ref[WINDOW:]


def attention_grads(first, doc_lengths, queries, prev_keys, keys, prev_values, values, grad_attn):
    count, width = queries.shape
    pairs = width // LANES
    ext = count + WINDOW
    tiles = count // QT
    column = lambda n: pl.BlockSpec((n, LANES), lambda i: (0, i))
    docs = doc_lengths.shape[0]
    return pl.pallas_call(
        attention_kernel,
        grid=(pairs,),
        in_specs=[
            pl.BlockSpec(memory_space=pltpu.SMEM),
            pl.BlockSpec((1, docs), lambda i: (0, 0)),
            column(count), column(WINDOW), column(count), column(WINDOW), column(count), column(count),
        ],
        out_specs=[column(count), column(WINDOW), column(WINDOW), column(count), column(count)],
        out_shape=[
            jax.ShapeDtypeStruct((count, width), BF16),
            jax.ShapeDtypeStruct((WINDOW, width), BF16),
            jax.ShapeDtypeStruct((WINDOW, width), BF16),
            jax.ShapeDtypeStruct((count, width), F32),
            jax.ShapeDtypeStruct((count, width), F32),
        ],
        scratch_shapes=[
            pltpu.VMEM((tiles, KT, QT), F32),
            pltpu.VMEM((ext, LANES), BF16),
            pltpu.VMEM((ext, LANES), BF16),
            pltpu.VMEM((ext, LANES), F32),
            pltpu.VMEM((ext, LANES), F32),
        ],
        compiler_params=params(),
        cost_estimate=pl.CostEstimate(
            flops=10 * count * KT * width, bytes_accessed=20 * count * width,
            transcendentals=count * KT * width // HD,
        ),
        name="attention",
    )(first, doc_lengths.reshape(1, docs), queries, prev_keys, keys, prev_values, values, grad_attn)


PACK = 256


def finish_kernel(
    dq_ref, dk_ref, dv_ref, bk_ref, bv_ref, wq_ref, wk_ref, wv_ref,
    hidden_ref, gain_ref, out_ref, slot_ref, gh_ref, sent_ref,
):
    count = hidden_ref.shape[0]
    grad_k = (dk_ref[...] + bk_ref[...].astype(F32)).astype(BF16)
    grad_v = (dv_ref[...] + bv_ref[...].astype(F32)).astype(BF16)
    norm = dot(dq_ref[...], wq_ref[...], 1, 1)
    norm = norm + dot(grad_k, wk_ref[...], 1, 1)
    norm = norm + dot(grad_v, wv_ref[...], 1, 1)
    full = hidden_ref[...].astype(F32)
    inverse = lax.rsqrt(jnp.mean(full * full, axis=1, keepdims=True) + EPS)
    unit = full * inverse
    scaled = norm * gain_ref[...]
    through = inverse * (scaled - unit * jnp.mean(scaled * unit, axis=1, keepdims=True))
    grad_hidden = (out_ref[...].astype(F32) + through).astype(BF16)
    gh_ref[...] = grad_hidden
    slots = sent_ref.shape[0]
    for at in range(0, slots, PACK):
        place = at + iota((PACK, count), 0)
        hit = place == slot_ref[0:1, :]
        for table in range(1, NG):
            hit = hit | (place == slot_ref[table : table + 1, :])
        sent_ref[at : at + PACK, :] = dot(
            jnp.where(hit, 1.0, 0.0).astype(BF16), grad_hidden, 1, 0
        ).astype(BF16)


def finish(dq, dk, dv, bk, bv, wq, wk, wv, hidden, gain, grad_out, slot, devices):
    count, width = hidden.shape
    places = devices * NG * SLOTS
    return pl.pallas_call(
        finish_kernel,
        out_shape=(
            jax.ShapeDtypeStruct((count, width), BF16),
            jax.ShapeDtypeStruct((places, width), BF16),
        ),
        compiler_params=params(),
        name="finish",
    )(dq, dk, dv, bk, bv, wq, wk, wv, hidden, gain.reshape(1, width), grad_out, slot)


COLLECT = 512


def collect_kernel(label_ref, rows_ref, out_ref):
    place = pl.program_id(1) * COLLECT + iota((COLLECT, label_ref.shape[2]), 0)
    hit = jnp.where(place == label_ref[0], 1.0, 0.0).astype(BF16)
    out_ref[0] = dot(hit, rows_ref[0], 1, 0).astype(BF16)


def collect(labels, rows):
    tables, number, width = rows.shape
    return pl.pallas_call(
        collect_kernel,
        grid=(tables, ROWS_DEV // COLLECT),
        in_specs=[
            pl.BlockSpec((1, 1, number), lambda t, i: (t, 0, 0)),
            pl.BlockSpec((1, number, width), lambda t, i: (t, 0, 0)),
        ],
        out_specs=pl.BlockSpec((1, COLLECT, width), lambda t, i: (t, i, 0)),
        out_shape=jax.ShapeDtypeStruct((tables, ROWS_DEV, width), BF16),
        compiler_params=params(),
        name="collect",
    )(labels, rows)


def exchanged(part):
    return lax.all_to_all(part, AXES, split_axis=0, concat_axis=0, tiled=True)


def shards(
    hidden,
    gain,
    queries,
    keys,
    values,
    w_query,
    w_key,
    w_value,
    w_out,
    grad_out,
    doc_lengths,
    hash_ids,
):
    count, width = hidden.shape
    devices = lax.axis_size(AXES)
    first = (lax.axis_index(AXES) * count).astype(I32).reshape(1)
    prev_keys, prev_values = shifted((keys, values), 1)
    slot, labels = make_slots(hash_ids, devices)
    labels = exchanged(labels.reshape(devices, NG, SLOTS))
    labels = jnp.transpose(labels, (1, 0, 2)).reshape(NG, 1, devices * SLOTS)
    grad_attn = dot(grad_out, w_out, 1, 1).astype(BF16)
    dq, dkp, dvp, dko, dvo = attention_grads(
        first, doc_lengths, queries, prev_keys, keys, prev_values, values, grad_attn
    )
    back_keys, back_values = shifted((dkp, dvp), -1)
    grad_hidden, sent = finish(
        dq, dko, dvo, back_keys, back_values, w_query, w_key, w_value,
        hidden, gain, grad_out, slot, devices,
    )
    rows = exchanged(sent.reshape(devices, NG, SLOTS, width))
    rows = jnp.transpose(rows, (1, 0, 2, 3)).reshape(NG, devices * SLOTS, width)
    return grad_hidden, collect(labels, rows)


def solution(mesh):
    spread = P(AXES, None)
    return jax.shard_map(
        shards,
        mesh=mesh,
        in_specs=(
            spread, P(), spread, spread, spread, P(), P(), P(), P(), spread, P(), P(None, AXES),
        ),
        out_specs=(spread, P(None, AXES, None)),
        check_vma=False,
    )
```

```python
import functools

import jax
import jax.numpy as jnp
from jax import lax
from jax.experimental import pallas as pl
from jax.experimental.pallas import tpu as pltpu
from jax.sharding import PartitionSpec as P

HD = 64
WINDOW = 512
NG = 2
ROWS_DEV = 2048
SLOTS = 5
EPS = 1e-06
NEG = -1e30
AXES = ("seq", "table")
LANES = 128
BF16 = jnp.bfloat16
F32 = jnp.float32
I32 = jnp.int32
GROUPS = (3, 3)


def iota(shape, dim):
    return lax.broadcasted_iota(I32, shape, dim)


def dot(left, right, left_dim, right_dim):
    return lax.dot_general(
        left, right, (((left_dim,), (right_dim,)), ((), ())), preferred_element_type=F32
    )


def params(mib):
    return pltpu.CompilerParams(vmem_limit_bytes=mib * 1024 * 1024)


def shifted(shard, by):
    count = lax.axis_size(AXES)
    pairs = [(i, i + by) for i in range(count) if 0 <= i + by < count]
    return lax.ppermute(shard, AXES, pairs)


MAIN = 4
CHUNK = 64


def slots_kernel(first_ref, row_ref, col_ref, slot_ref, label_ref):
    count = row_ref.shape[1]
    places = label_ref.shape[1]
    odd = lax.rem(first_ref[0] // count, 2)
    labels = jnp.full((1, places), ROWS_DEV, I32)
    sub = iota((count, count), 0)
    lane = iota((count, count), 1)
    for table in range(NG):
        row = row_ref[table : table + 1, :]
        col = col_ref[:, table : table + 1]
        same = col == row
        first_col = jnp.sum((same & (lane < sub)).astype(I32), axis=1, keepdims=True) == 0
        first_row = jnp.sum((same & (sub < lane)).astype(I32), axis=0, keepdims=True) == 0
        row_owner = row // ROWS_DEV
        col_owner = col // ROWS_DEV
        mates = row_owner == col_owner
        place_row = jnp.sum((first_col & mates & (col < row)).astype(I32), axis=0, keepdims=True)
        place_col = jnp.sum((first_row & mates & (row < col)).astype(I32), axis=1, keepdims=True)
        side = lax.rem(table + odd, 2)
        main = row_owner * (NG * MAIN) + side * MAIN + place_row
        slot_ref[table : table + 1, :] = jnp.where(place_row < MAIN, main, -1)
        last = row_owner * NG + table
        slot_ref[NG + table : NG + table + 1, :] = jnp.where(place_row < MAIN, -1, last)
        slot_col = col_owner * (NG * SLOTS) + table * SLOTS + place_col
        local_col = col - col_owner * ROWS_DEV
        hit = slot_col == iota((count, places), 1)
        labels = jnp.minimum(
            labels, jnp.min(jnp.where(hit, local_col, ROWS_DEV), axis=0, keepdims=True)
        )
    label_ref[...] = labels


def make_slots(first, hash_ids, devices):
    count = hash_ids.shape[1]
    places = devices * NG * SLOTS
    return pl.pallas_call(
        slots_kernel,
        in_specs=[
            pl.BlockSpec(memory_space=pltpu.SMEM),
            pl.BlockSpec(memory_space=pltpu.VMEM),
            pl.BlockSpec(memory_space=pltpu.VMEM),
        ],
        out_shape=(
            jax.ShapeDtypeStruct((2 * NG, count), I32),
            jax.ShapeDtypeStruct((1, places), I32),
        ),
        compiler_params=params(56),
        name="slots",
    )(first, hash_ids, jnp.transpose(hash_ids))


QT = 256
KT = QT + WINDOW


def attention_kernel(
    first_ref, len_ref, q_ref, kp_ref, ko_ref, vp_ref, vo_ref, da_ref,
    dq_ref, back_ref, dko_ref, dvo_ref,
    bias_ref, kx_ref, vx_ref, dk_ref, dv_ref,
):
    count = q_ref.shape[0]
    tiles = count // QT

    @pl.when(pl.program_id(0) == 0)
    def _():
        docs = len_ref.shape[1]
        first = first_ref[0]
        upto = iota((docs, docs), 1) <= iota((docs, docs), 0)
        ends = jnp.sum(jnp.where(upto, len_ref[...], 0), axis=1, keepdims=True)
        qpos = first + iota((1, count), 1)
        start = jnp.max(jnp.where(ends <= qpos, ends, 0), axis=0, keepdims=True)
        low = jnp.maximum(start, qpos - (WINDOW - 1))
        for tile in range(tiles):
            cols = slice(tile * QT, (tile + 1) * QT)
            kpos = first - WINDOW + tile * QT + iota((KT, QT), 0)
            ok = (kpos >= low[:, cols]) & (kpos <= qpos[:, cols])
            bias_ref[tile] = jnp.where(ok, 0.0, NEG)

    kx_ref[:WINDOW] = kp_ref[0]
    kx_ref[WINDOW:] = ko_ref[...]
    vx_ref[:WINDOW] = vp_ref[0]
    vx_ref[WINDOW:] = vo_ref[...]
    lane = iota((QT, LANES), 1)
    scale = HD ** (-0.5)
    zero = jnp.zeros((QT, LANES), BF16)
    for tile in range(tiles):
        rows = slice(tile * QT, (tile + 1) * QT)
        span = slice(tile * QT, tile * QT + KT)
        q = q_ref[rows, :] * jnp.asarray(scale, BF16)
        da = da_ref[rows, :]
        k = kx_ref[span, :]
        v = vx_ref[span, :]
        dq = dk = dv = None
        for half in range(LANES // HD):
            mine = (lane // HD) == half
            qh = jnp.where(mine, q, zero)
            dah = jnp.where(mine, da, zero)
            score = dot(k, qh, 1, 1) + bias_ref[tile]
            top = jnp.max(score, axis=0, keepdims=True)
            expo = jnp.exp(score - top)
            total = jnp.sum(expo, axis=0, keepdims=True)
            prob = expo * (1.0 / total)
            lowprob = prob.astype(BF16)
            dprob = dot(v, dah, 1, 1)
            delta = jnp.sum(lowprob.astype(F32) * dprob, axis=0, keepdims=True)
            dscore = (prob * (dprob - delta)).astype(BF16)
            dvh = dot(lowprob, dah, 1, 0)
            dkh = dot(dscore, qh, 1, 0)
            dqh = jnp.where(mine, dot(dscore, k, 0, 0), 0.0)
            dv = dvh if dv is None else dv + dvh
            dk = dkh if dk is None else dk + dkh
            dq = dqh if dq is None else dq + dqh
        dq_ref[rows, :] = (dq * scale).astype(BF16)
        if tile == 0:
            dk_ref[span, :] = dk
            dv_ref[span, :] = dv
        else:
            seen = slice(tile * QT, (tile - 1) * QT + KT)
            fresh = slice((tile - 1) * QT + KT, tile * QT + KT)
            both = KT - QT
            dk_ref[seen, :] += dk[:both]
            dv_ref[seen, :] += dv[:both]
            dk_ref[fresh, :] = dk[both:]
            dv_ref[fresh, :] = dv[both:]
    back_ref[0] = dk_ref[:WINDOW].astype(BF16)
    back_ref[1] = dv_ref[:WINDOW].astype(BF16)
    dko_ref[...] = dk_ref[WINDOW:]
    dvo_ref[...] = dv_ref[WINDOW:]


def attention_grads(first, doc_lengths, queries, halo, keys, values, grad_attn, at):
    count = queries.shape[0]
    width = halo.shape[2]
    pairs = width // LANES
    ext = count + WINDOW
    tiles = count // QT
    column = pl.BlockSpec((count, LANES), lambda i: (0, i + at))
    fresh = pl.BlockSpec((count, LANES), lambda i: (0, i))
    docs = doc_lengths.shape[0]
    return pl.pallas_call(
        attention_kernel,
        grid=(pairs,),
        in_specs=[
            pl.BlockSpec(memory_space=pltpu.SMEM),
            pl.BlockSpec((1, docs), lambda i: (0, 0)),
            column,
            pl.BlockSpec((1, WINDOW, LANES), lambda i: (0, 0, i)),
            column,
            pl.BlockSpec((1, WINDOW, LANES), lambda i: (1, 0, i)),
            column,
            column,
        ],
        out_specs=[fresh, pl.BlockSpec((2, WINDOW, LANES), lambda i: (0, 0, i)), fresh, fresh],
        out_shape=[
            jax.ShapeDtypeStruct((count, width), BF16),
            jax.ShapeDtypeStruct((2, WINDOW, width), BF16),
            jax.ShapeDtypeStruct((count, width), F32),
            jax.ShapeDtypeStruct((count, width), F32),
        ],
        scratch_shapes=[
            pltpu.VMEM((tiles, KT, QT), F32),
            pltpu.VMEM((ext, LANES), BF16),
            pltpu.VMEM((ext, LANES), BF16),
            pltpu.VMEM((ext, LANES), F32),
            pltpu.VMEM((ext, LANES), F32),
        ],
        compiler_params=params(56),
        cost_estimate=pl.CostEstimate(
            flops=10 * count * KT * width, bytes_accessed=20 * count * width,
            transcendentals=count * KT * width // HD,
        ),
        name="attention",
    )(first, doc_lengths.reshape(1, docs), queries, halo, keys, halo, values, grad_attn)


PACK = 32


def finish_kernel(*refs):
    groups = len(GROUPS)
    parts = [refs[4 * g : 4 * g + 4] for g in range(groups)]
    (wq_ref, wk_ref, wv_ref, hidden_ref, gain_ref, out_ref, slot_ref, gh_ref, sent_ref) = refs[
        4 * groups :
    ]
    count, width = hidden_ref.shape
    grad_q = jnp.concatenate([dq[...] for dq, _, _, _ in parts], axis=1)
    grad_k = jnp.concatenate(
        [(dk[...] + back[0].astype(F32)).astype(BF16) for _, back, dk, _ in parts], axis=1
    )
    grad_v = jnp.concatenate(
        [(dv[...] + back[1].astype(F32)).astype(BF16) for _, back, _, dv in parts], axis=1
    )
    norm = dot(grad_q, wq_ref[...], 1, 1)
    norm = norm + dot(grad_k, wk_ref[...], 1, 1)
    norm = norm + dot(grad_v, wv_ref[...], 1, 1)
    full = hidden_ref[...].astype(F32)
    inverse = lax.rsqrt(jnp.mean(full * full, axis=1, keepdims=True) + EPS)
    unit = full * inverse
    scaled = norm * gain_ref[...]
    through = inverse * (scaled - unit * jnp.mean(scaled * unit, axis=1, keepdims=True))
    grad_hidden = (out_ref[...].astype(F32) + through).astype(BF16)
    gh_ref[...] = grad_hidden

    def hits(place, at):
        hit = place == slot_ref[at : at + 1, :]
        for table in range(1, NG):
            hit = hit | (place == slot_ref[at + table : at + table + 1, :])
        return jnp.where(hit, 1.0, 0.0).astype(BF16)

    blocks = width // LANES
    both = NG * MAIN
    tail = CHUNK - blocks * both
    cut = lambda value, c: value[:, c * LANES : (c + 1) * LANES]
    for at in range(0, sent_ref.shape[0], PACK):
        place = at * both + iota((PACK * both, count), 0)
        main = dot(hits(place, 0), grad_hidden, 1, 0)
        for c in range(0, blocks, 2):
            pair = [cut(main, c + i).reshape(PACK, both, LANES) for i in range(2)]
            sent_ref[at : at + PACK, c * both : (c + 2) * both, :] = jnp.concatenate(
                pair, axis=1
            ).astype(BF16)
        rows = iota((PACK * tail, count), 0)
        place = (at + rows // tail) * NG + lax.rem(rows, NG)
        last = dot(hits(place, NG), grad_hidden, 1, 0)
        block = lax.rem(iota((PACK * tail, LANES), 0), tail) // NG
        value = jnp.zeros((PACK * tail, LANES), F32)
        for c in range(blocks):
            value = jnp.where(block == c, cut(last, c), value)
        sent_ref[at : at + PACK, blocks * both :, :] = value.reshape(PACK, tail, LANES).astype(BF16)


def finish(parts, wq, wk, wv, hidden, gain, grad_out, slot, devices):
    count, width = hidden.shape
    return pl.pallas_call(
        finish_kernel,
        out_shape=(
            jax.ShapeDtypeStruct((count, width), BF16),
            jax.ShapeDtypeStruct((devices, CHUNK, LANES), BF16),
        ),
        compiler_params=params(56),
        name="finish",
    )(
        *[array for part in parts for array in part],
        wq, wk, wv, hidden, gain.reshape(1, width), grad_out, slot,
    )


COLLECT = 512
APART = 16


def collect_kernel(label_ref, got_ref, out_ref, rows_ref):
    devices = got_ref.shape[0]
    blocks = rows_ref.shape[2] // LANES
    both = NG * MAIN
    tail = CHUNK - blocks * both
    mains = devices * MAIN

    @pl.when((pl.program_id(0) == 0) & (pl.program_id(1) == 0))
    def _():
        low = iota((devices // 2, both, LANES), 1) < MAIN
        for c in range(0, blocks, 2):
            wide = got_ref[:, c * both : (c + 2) * both, :].astype(F32)
            for i in range(2):
                cols = slice((c + i) * LANES, (c + i + 1) * LANES)
                piece = wide[:, i * both : (i + 1) * both, :]
                piece = piece.reshape(devices // 2, 2, both, LANES)
                even, odd = piece[:, 0], piece[:, 1]
                zero = jnp.where(low, even, odd).reshape(mains, LANES)
                one = jnp.where(low, odd, even).reshape(mains, LANES)
                rows_ref[0, :mains, cols] = zero.astype(BF16)
                rows_ref[1, :mains, cols] = one.astype(BF16)
        shape = (NG * blocks * APART, APART * tail)
        row = iota((shape[0], 1), 0)
        device = lax.rem(row, APART)
        block = lax.rem(row // APART, blocks)
        table = row // (APART * blocks)
        source = device * tail + block * NG + table
        pick = jnp.where(source == iota(shape, 1), 1.0, 0.0).astype(BF16)
        for at in range(0, devices, APART):
            rest = got_ref[at : at + APART, blocks * both :, :].reshape(APART * tail, LANES)
            rest = dot(pick, rest, 1, 0).astype(BF16)
            for t in range(NG):
                for c in range(blocks):
                    start = (t * blocks + c) * APART
                    rows_ref[t, mains + at : mains + at + APART, c * LANES : (c + 1) * LANES] = rest[
                        start : start + APART
                    ]

    place = pl.program_id(1) * COLLECT + iota((COLLECT, label_ref.shape[2]), 0)
    hit = jnp.where(place == label_ref[0], 1.0, 0.0).astype(BF16)
    out_ref[0] = dot(hit, rows_ref[pl.program_id(0)], 1, 0).astype(BF16)


def collect(labels, got, width):
    tables, _, number = labels.shape
    return pl.pallas_call(
        collect_kernel,
        grid=(tables, ROWS_DEV // COLLECT),
        in_specs=[
            pl.BlockSpec((1, 1, number), lambda t, i: (t, 0, 0)),
            pl.BlockSpec(got.shape, lambda t, i: (0, 0, 0)),
        ],
        out_specs=pl.BlockSpec((1, COLLECT, width), lambda t, i: (t, i, 0)),
        out_shape=jax.ShapeDtypeStruct((tables, ROWS_DEV, width), BF16),
        scratch_shapes=[pltpu.VMEM((tables, number, width), BF16)],
        compiler_params=params(56),
        name="collect",
    )(labels, got)


def exchanged(part):
    return lax.all_to_all(part, AXES, split_axis=0, concat_axis=0, tiled=True)


def shards(
    hidden,
    gain,
    queries,
    keys,
    values,
    w_query,
    w_key,
    w_value,
    w_out,
    grad_out,
    doc_lengths,
    hash_ids,
):
    count, width = hidden.shape
    devices = lax.axis_size(AXES)
    first = (lax.axis_index(AXES) * count).astype(I32).reshape(1)
    halos = []
    at = 0
    for pairs in GROUPS:
        cols = slice(at * LANES, (at + pairs) * LANES)
        halos.append(shifted(jnp.stack([keys[:, cols], values[:, cols]]), 1))
        at += pairs
    grad_attn = dot(grad_out, w_out, 1, 1).astype(BF16)
    slot, labels = make_slots(first, hash_ids, devices)
    grad_attn, slot, labels = lax.optimization_barrier((grad_attn, slot, labels))
    parts = []
    at = 0
    for pairs, halo in zip(GROUPS, halos):
        dq, back, dk, dv = attention_grads(
            first, doc_lengths, queries, halo, keys, values, grad_attn, at
        )
        parts.append((dq, shifted(back, -1), dk, dv))
        at += pairs
    labels, _ = lax.optimization_barrier((labels, parts[-1][0]))
    labels = exchanged(labels.reshape(devices, NG, SLOTS))
    labels = jnp.transpose(labels, (1, 0, 2))
    main = labels[:, :, :MAIN].reshape(NG, devices // 2, 2, MAIN)
    main = jnp.stack([main[0], main[1, :, ::-1]])
    labels = jnp.concatenate([main.reshape(NG, devices * MAIN), labels[:, :, MAIN]], axis=1)
    grad_hidden, sent = finish(
        parts, w_query, w_key, w_value, hidden, gain, grad_out, slot, devices
    )
    return grad_hidden, collect(labels[:, None, :], exchanged(sent), width)


def solution(mesh):
    spread = P(AXES, None)
    return jax.shard_map(
        shards,
        mesh=mesh,
        in_specs=(
            spread, P(), spread, spread, spread, P(), P(), P(), P(), spread, P(), P(None, AXES),
        ),
        out_specs=(spread, P(None, AXES, None)),
        check_vma=False,
    )
```

```python
import functools

import jax
import jax.numpy as jnp
from jax import lax
from jax.experimental import pallas as pl
from jax.experimental.pallas import tpu as pltpu
from jax.sharding import PartitionSpec as P

HD = 64
WINDOW = 512
NG = 2
ROWS_DEV = 2048
SLOTS = 5
EPS = 1e-06
NEG = -1e30
AXES = ("seq", "table")
LANES = 128
BF16 = jnp.bfloat16
F32 = jnp.float32
I32 = jnp.int32
GROUPS = (3, 3)


def iota(shape, dim):
    return lax.broadcasted_iota(I32, shape, dim)


def dot(left, right, left_dim, right_dim):
    return lax.dot_general(
        left, right, (((left_dim,), (right_dim,)), ((), ())), preferred_element_type=F32
    )


def params(mib):
    return pltpu.CompilerParams(vmem_limit_bytes=mib * 1024 * 1024)


def shifted(shard, by):
    count = lax.axis_size(AXES)
    pairs = [(i, i + by) for i in range(count) if 0 <= i + by < count]
    return lax.ppermute(shard, AXES, pairs)


MAIN = 4
CHUNK = 64


def slots_kernel(first_ref, row_ref, col_ref, slot_ref, label_ref):
    count = row_ref.shape[1]
    places = label_ref.shape[1]
    odd = lax.rem(first_ref[0] // count, 2)
    labels = jnp.full((1, places), ROWS_DEV, I32)
    sub = iota((count, count), 0)
    lane = iota((count, count), 1)
    for table in range(NG):
        row = row_ref[table : table + 1, :]
        col = col_ref[:, table : table + 1]
        same = col == row
        first_col = jnp.sum((same & (lane < sub)).astype(I32), axis=1, keepdims=True) == 0
        first_row = jnp.sum((same & (sub < lane)).astype(I32), axis=0, keepdims=True) == 0
        row_owner = row // ROWS_DEV
        col_owner = col // ROWS_DEV
        mates = row_owner == col_owner
        place_row = jnp.sum((first_col & mates & (col < row)).astype(I32), axis=0, keepdims=True)
        place_col = jnp.sum((first_row & mates & (row < col)).astype(I32), axis=1, keepdims=True)
        side = lax.rem(table + odd, 2)
        main = row_owner * (NG * MAIN) + side * MAIN + place_row
        slot_ref[table : table + 1, :] = jnp.where(place_row < MAIN, main, -1)
        last = row_owner * NG + table
        slot_ref[NG + table : NG + table + 1, :] = jnp.where(place_row < MAIN, -1, last)
        slot_col = col_owner * (NG * SLOTS) + table * SLOTS + place_col
        local_col = col - col_owner * ROWS_DEV
        hit = slot_col == iota((count, places), 1)
        labels = jnp.minimum(
            labels, jnp.min(jnp.where(hit, local_col, ROWS_DEV), axis=0, keepdims=True)
        )
    label_ref[...] = labels


def make_slots(first, hash_ids, devices):
    count = hash_ids.shape[1]
    places = devices * NG * SLOTS
    return pl.pallas_call(
        slots_kernel,
        in_specs=[
            pl.BlockSpec(memory_space=pltpu.SMEM),
            pl.BlockSpec(memory_space=pltpu.VMEM),
            pl.BlockSpec(memory_space=pltpu.VMEM),
        ],
        out_shape=(
            jax.ShapeDtypeStruct((2 * NG, count), I32),
            jax.ShapeDtypeStruct((1, places), I32),
        ),
        compiler_params=params(56),
        name="slots",
    )(first, hash_ids, jnp.transpose(hash_ids))


QT = 256
KT = QT + WINDOW


def attention_kernel(
    first_ref, len_ref, q_ref, kp_ref, ko_ref, vp_ref, vo_ref, da_ref,
    dq_ref, back_ref, dko_ref, dvo_ref,
    bias_ref, kx_ref, vx_ref, dk_ref, dv_ref,
):
    count = q_ref.shape[0]
    tiles = count // QT

    @pl.when(pl.program_id(0) == 0)
    def _():
        docs = len_ref.shape[1]
        first = first_ref[0]
        upto = iota((docs, docs), 1) <= iota((docs, docs), 0)
        ends = jnp.sum(jnp.where(upto, len_ref[...], 0), axis=1, keepdims=True)
        qpos = first + iota((1, count), 1)
        start = jnp.max(jnp.where(ends <= qpos, ends, 0), axis=0, keepdims=True)
        low = jnp.maximum(start, qpos - (WINDOW - 1))
        for tile in range(tiles):
            cols = slice(tile * QT, (tile + 1) * QT)
            kpos = first - WINDOW + tile * QT + iota((KT, QT), 0)
            ok = (kpos >= low[:, cols]) & (kpos <= qpos[:, cols])
            bias_ref[tile] = jnp.where(ok, 0.0, NEG)

    kx_ref[:WINDOW] = kp_ref[0]
    kx_ref[WINDOW:] = ko_ref[...]
    vx_ref[:WINDOW] = vp_ref[0]
    vx_ref[WINDOW:] = vo_ref[...]
    lane = iota((QT, LANES), 1)
    scale = HD ** (-0.5)
    zero = jnp.zeros((QT, LANES), BF16)
    steps = [(tile, half) for tile in range(tiles) for half in range(LANES // HD)]
    rowlane = iota((LANES, QT), 0)

    def open_step(step):
        tile, half = step
        rows = slice(tile * QT, (tile + 1) * QT)
        span = slice(tile * QT, tile * QT + KT)
        mine = (lane // HD) == half
        qh = jnp.where(mine, q_ref[rows, :] * jnp.asarray(scale, BF16), zero)
        dah = jnp.where(mine, da_ref[rows, :], zero)
        score = dot(kx_ref[span, :], qh, 1, 1) + bias_ref[tile]
        dprob = dot(vx_ref[span, :], dah, 1, 1)
        return qh, dah, score, dprob

    opened = {steps[0]: open_step(steps[0])}
    held = {}
    for n, step in enumerate(steps):
        tile, half = step
        rows = slice(tile * QT, (tile + 1) * QT)
        span = slice(tile * QT, tile * QT + KT)
        if n + 1 < len(steps):
            opened[steps[n + 1]] = open_step(steps[n + 1])
        qh, dah, score, dprob = opened.pop(step)
        top = jnp.max(score, axis=0, keepdims=True)
        expo = jnp.exp(score - top)
        total = jnp.sum(expo, axis=0, keepdims=True)
        prob = expo * (1.0 / total)
        lowprob = prob.astype(BF16)
        delta = jnp.sum(prob * dprob, axis=0, keepdims=True)
        dscore = (prob * (dprob - delta)).astype(BF16)
        dqh = jnp.where((rowlane // HD) == half, dot(kx_ref[span, :], dscore, 0, 0), 0.0)
        if half == 0:
            held = dict(lp=lowprob, ds=dscore, q=qh, da=dah, dq=dqh)
            continue
        dq = held["dq"] + dqh
        dv = dot(jnp.concatenate([held["lp"], lowprob], axis=1), jnp.concatenate([held["da"], dah], axis=0), 1, 0)
        dk = dot(jnp.concatenate([held["ds"], dscore], axis=1), jnp.concatenate([held["q"], qh], axis=0), 1, 0)
        dq_ref[rows, :] = jnp.transpose(dq * scale).astype(BF16)
        if tile == 0:
            dk_ref[span, :] = dk
            dv_ref[span, :] = dv
        else:
            seen = slice(tile * QT, (tile - 1) * QT + KT)
            fresh = slice((tile - 1) * QT + KT, tile * QT + KT)
            both = KT - QT
            dk_ref[seen, :] += dk[:both]
            dv_ref[seen, :] += dv[:both]
            dk_ref[fresh, :] = dk[both:]
            dv_ref[fresh, :] = dv[both:]
    back_ref[0] = dk_ref[:WINDOW].astype(BF16)
    back_ref[1] = dv_ref[:WINDOW].astype(BF16)
    dko_ref[...] = dk_ref[WINDOW:]
    dvo_ref[...] = dv_ref[WINDOW:]


def attention_grads(first, doc_lengths, queries, halo, keys, values, grad_attn, at):
    count = queries.shape[0]
    width = halo.shape[2]
    pairs = width // LANES
    ext = count + WINDOW
    tiles = count // QT
    column = pl.BlockSpec((count, LANES), lambda i: (0, i + at))
    fresh = pl.BlockSpec((count, LANES), lambda i: (0, i))
    docs = doc_lengths.shape[0]
    return pl.pallas_call(
        attention_kernel,
        grid=(pairs,),
        in_specs=[
            pl.BlockSpec(memory_space=pltpu.SMEM),
            pl.BlockSpec((1, docs), lambda i: (0, 0)),
            column,
            pl.BlockSpec((1, WINDOW, LANES), lambda i: (0, 0, i)),
            column,
            pl.BlockSpec((1, WINDOW, LANES), lambda i: (1, 0, i)),
            column,
            column,
        ],
        out_specs=[fresh, pl.BlockSpec((2, WINDOW, LANES), lambda i: (0, 0, i)), fresh, fresh],
        out_shape=[
            jax.ShapeDtypeStruct((count, width), BF16),
            jax.ShapeDtypeStruct((2, WINDOW, width), BF16),
            jax.ShapeDtypeStruct((count, width), F32),
            jax.ShapeDtypeStruct((count, width), F32),
        ],
        scratch_shapes=[
            pltpu.VMEM((tiles, KT, QT), F32),
            pltpu.VMEM((ext, LANES), BF16),
            pltpu.VMEM((ext, LANES), BF16),
            pltpu.VMEM((ext, LANES), F32),
            pltpu.VMEM((ext, LANES), F32),
        ],
        compiler_params=params(56),
        cost_estimate=pl.CostEstimate(
            flops=10 * count * KT * width, bytes_accessed=20 * count * width,
            transcendentals=count * KT * width // HD,
        ),
        name="attention",
    )(first, doc_lengths.reshape(1, docs), queries, halo, keys, halo, values, grad_attn)


PACK = 32
SPREAD = 16


def finish_kernel(*refs):
    groups = len(GROUPS)
    parts = [refs[4 * g : 4 * g + 4] for g in range(groups)]
    (
        wq_in, wk_in, wv_in, hidden_in, out_in, gain_ref, slot_ref, gh_out, sent_out,
        dq_ref, dk_ref, dv_ref, back_ref, wq_ref, wk_ref, wv_ref, hidden_ref, out_ref,
        gh_ref, sent_ref, sems,
    ) = refs[4 * groups :]
    count, width = hidden_ref.shape
    devices = sent_ref.shape[0]
    started = []

    def bring(*pairs):
        copies = []
        for source, target in pairs:
            copies.append(pltpu.make_async_copy(source, target, sems.at[len(started)]))
            started.append(copies[-1])
            copies[-1].start()
        return copies

    def arrive(copies):
        for copy in copies:
            copy.wait()

    spans = []
    at = 0
    for pairs in GROUPS:
        spans.append(slice(at * LANES, (at + pairs) * LANES))
        at += pairs
    need_hidden = bring((hidden_in, hidden_ref))
    need_q = bring(*[(p[0], dq_ref.at[:, c]) for p, c in zip(parts, spans)], (wq_in, wq_ref))
    need_k = bring(
        *[(p[1].at[0], back_ref.at[0, :, c]) for p, c in zip(parts, spans)],
        *[(p[2], dk_ref.at[:, c]) for p, c in zip(parts, spans)],
        (wk_in, wk_ref),
    )
    need_v = bring(
        *[(p[1].at[1], back_ref.at[1, :, c]) for p, c in zip(parts, spans)],
        *[(p[3], dv_ref.at[:, c]) for p, c in zip(parts, spans)],
        (wv_in, wv_ref),
    )
    need_out = bring((out_in, out_ref))

    def hits(place, at):
        hit = place == slot_ref[at : at + 1, :]
        for table in range(1, NG):
            hit = hit | (place == slot_ref[at + table : at + table + 1, :])
        return jnp.where(hit, 1.0, 0.0).astype(BF16)

    blocks = width // LANES
    both = NG * MAIN
    tail = CHUNK - blocks * both
    shape = (SPREAD * tail, blocks * SPREAD * NG)
    row = iota((shape[0], 1), 0)
    inner = lax.rem(row, tail)
    source = (inner // NG) * (SPREAD * NG) + (row // tail) * NG + lax.rem(inner, NG)
    lay = jnp.where((inner < blocks * NG) & (source == iota(shape, 1)), 1.0, 0.0).astype(BF16)

    arrive(need_hidden)
    full = hidden_ref[...].astype(F32)
    inverse = lax.rsqrt(jnp.mean(full * full, axis=1, keepdims=True) + EPS)
    arrive(need_q)
    norm = dot(dq_ref[...], wq_ref[...], 1, 1)
    arrive(need_k)
    norm = norm + dot((dk_ref[...] + back_ref[0].astype(F32)).astype(BF16), wk_ref[...], 1, 1)
    arrive(need_v)
    norm = norm + dot((dv_ref[...] + back_ref[1].astype(F32)).astype(BF16), wv_ref[...], 1, 1)
    arrive(need_out)
    unit = hidden_ref[...].astype(F32) * inverse
    scaled = norm * gain_ref[...]
    through = inverse * (scaled - unit * jnp.mean(scaled * unit, axis=1, keepdims=True))
    grad_hidden = (out_ref[...].astype(F32) + through).astype(BF16)
    gh_ref[...] = grad_hidden
    leaving = bring((gh_ref, gh_out))

    cut = lambda value, c: value[:, c * LANES : (c + 1) * LANES]
    rest = dot(hits(iota((devices * NG, count), 0), NG), grad_hidden, 1, 0).astype(BF16)
    for at in range(0, devices, PACK):
        place = at * both + iota((PACK * both, count), 0)
        main = dot(hits(place, 0), grad_hidden, 1, 0)
        for c in range(0, blocks, 2):
            pair = [cut(main, c + i).reshape(PACK, both, LANES) for i in range(2)]
            sent_ref[at : at + PACK, c * both : (c + 2) * both, :] = jnp.concatenate(
                pair, axis=1
            ).astype(BF16)
        for low in range(at, at + PACK, SPREAD):
            some = rest[low * NG : (low + SPREAD) * NG]
            some = jnp.concatenate([cut(some, c) for c in range(blocks)], axis=0)
            sent_ref[low : low + SPREAD, blocks * both :, :] = (
                dot(lay, some, 1, 0).reshape(SPREAD, tail, LANES).astype(BF16)
            )
        leaving += bring((sent_ref.at[at : at + PACK], sent_out.at[at : at + PACK]))
    arrive(leaving)


def finish(parts, wq, wk, wv, hidden, gain, grad_out, slot, devices):
    count, width = hidden.shape
    groups = len(GROUPS)
    place = pl.BlockSpec(memory_space=pl.ANY)
    small = pl.BlockSpec(memory_space=pltpu.VMEM)
    copies = 5 * groups + 6 + devices // PACK
    return pl.pallas_call(
        finish_kernel,
        in_specs=[place] * (4 * groups + 5) + [small] * 2,
        out_specs=(place, place),
        out_shape=(
            jax.ShapeDtypeStruct((count, width), BF16),
            jax.ShapeDtypeStruct((devices, CHUNK, LANES), BF16),
        ),
        scratch_shapes=[
            pltpu.VMEM((count, width), BF16),
            pltpu.VMEM((count, width), F32),
            pltpu.VMEM((count, width), F32),
            pltpu.VMEM((2, WINDOW, width), BF16),
            pltpu.VMEM((width, width), BF16),
            pltpu.VMEM((width, width), BF16),
            pltpu.VMEM((width, width), BF16),
            pltpu.VMEM((count, width), BF16),
            pltpu.VMEM((count, width), BF16),
            pltpu.VMEM((count, width), BF16),
            pltpu.VMEM((devices, CHUNK, LANES), BF16),
            pltpu.SemaphoreType.DMA((copies,)),
        ],
        compiler_params=params(56),
        name="finish",
    )(
        *[array for part in parts for array in part],
        wq, wk, wv, hidden, grad_out, gain.reshape(1, width), slot,
    )


COLLECT = 1024
APART = 16


def collect_kernel(label_ref, got_ref, out_ref, rows_ref):
    devices = got_ref.shape[0]
    blocks = rows_ref.shape[2] // LANES
    both = NG * MAIN
    tail = CHUNK - blocks * both
    mains = devices * MAIN

    @pl.when((pl.program_id(0) == 0) & (pl.program_id(1) == 0))
    def _():
        low = iota((devices // 2, both, LANES), 1) < MAIN
        for c in range(0, blocks, 2):
            wide = got_ref[:, c * both : (c + 2) * both, :].astype(F32)
            for i in range(2):
                cols = slice((c + i) * LANES, (c + i + 1) * LANES)
                piece = wide[:, i * both : (i + 1) * both, :]
                piece = piece.reshape(devices // 2, 2, both, LANES)
                even, odd = piece[:, 0], piece[:, 1]
                zero = jnp.where(low, even, odd).reshape(mains, LANES)
                one = jnp.where(low, odd, even).reshape(mains, LANES)
                rows_ref[0, :mains, cols] = zero.astype(BF16)
                rows_ref[1, :mains, cols] = one.astype(BF16)
        shape = (NG * blocks * APART, APART * tail)
        row = iota((shape[0], 1), 0)
        device = lax.rem(row, APART)
        block = lax.rem(row // APART, blocks)
        table = row // (APART * blocks)
        source = device * tail + block * NG + table
        pick = jnp.where(source == iota(shape, 1), 1.0, 0.0).astype(BF16)
        for at in range(0, devices, APART):
            rest = got_ref[at : at + APART, blocks * both :, :].reshape(APART * tail, LANES)
            rest = dot(pick, rest, 1, 0).astype(BF16)
            for t in range(NG):
                for c in range(blocks):
                    start = (t * blocks + c) * APART
                    rows_ref[t, mains + at : mains + at + APART, c * LANES : (c + 1) * LANES] = rest[
                        start : start + APART
                    ]

    place = pl.program_id(1) * COLLECT + iota((COLLECT, label_ref.shape[2]), 0)
    hit = jnp.where(place == label_ref[0], 1.0, 0.0).astype(BF16)
    out_ref[0] = dot(hit, rows_ref[pl.program_id(0)], 1, 0).astype(BF16)


def collect(labels, got, width):
    tables, _, number = labels.shape
    return pl.pallas_call(
        collect_kernel,
        grid=(tables, ROWS_DEV // COLLECT),
        in_specs=[
            pl.BlockSpec((1, 1, number), lambda t, i: (t, 0, 0)),
            pl.BlockSpec(got.shape, lambda t, i: (0, 0, 0)),
        ],
        out_specs=pl.BlockSpec((1, COLLECT, width), lambda t, i: (t, i, 0)),
        out_shape=jax.ShapeDtypeStruct((tables, ROWS_DEV, width), BF16),
        scratch_shapes=[pltpu.VMEM((tables, number, width), BF16)],
        compiler_params=params(56),
        name="collect",
    )(labels, got)


def exchanged(part):
    return lax.all_to_all(part, AXES, split_axis=0, concat_axis=0, tiled=True)


def shards(
    hidden,
    gain,
    queries,
    keys,
    values,
    w_query,
    w_key,
    w_value,
    w_out,
    grad_out,
    doc_lengths,
    hash_ids,
):
    count, width = hidden.shape
    devices = lax.axis_size(AXES)
    first = (lax.axis_index(AXES) * count).astype(I32).reshape(1)
    halos = []
    at = 0
    for pairs in GROUPS:
        cols = slice(at * LANES, (at + pairs) * LANES)
        halos.append(shifted(jnp.stack([keys[:, cols], values[:, cols]]), 1))
        at += pairs
    grad_attn = dot(grad_out, w_out, 1, 1).astype(BF16)
    slot, labels = make_slots(first, hash_ids, devices)
    grad_attn, slot, labels = lax.optimization_barrier((grad_attn, slot, labels))
    parts = []
    at = 0
    for pairs, halo in zip(GROUPS, halos):
        dq, back, dk, dv = attention_grads(
            first, doc_lengths, queries, halo, keys, values, grad_attn, at
        )
        parts.append((dq, shifted(back, -1), dk, dv))
        at += pairs
    labels, _ = lax.optimization_barrier((labels, parts[-1][0]))
    labels = exchanged(labels.reshape(devices, NG, SLOTS))
    labels = jnp.transpose(labels, (1, 0, 2))
    main = labels[:, :, :MAIN].reshape(NG, devices // 2, 2, MAIN)
    main = jnp.stack([main[0], main[1, :, ::-1]])
    labels = jnp.concatenate([main.reshape(NG, devices * MAIN), labels[:, :, MAIN]], axis=1)
    grad_hidden, sent = finish(
        parts, w_query, w_key, w_value, hidden, gain, grad_out, slot, devices
    )
    return grad_hidden, collect(labels[:, None, :], exchanged(sent), width)


def solution(mesh):
    spread = P(AXES, None)
    return jax.shard_map(
        shards,
        mesh=mesh,
        in_specs=(
            spread, P(), spread, spread, spread, P(), P(), P(), P(), spread, P(), P(None, AXES),
        ),
        out_specs=(spread, P(None, AXES, None)),
        check_vma=False,
    )
```

```python
import functools

import jax
import jax.numpy as jnp
from jax import lax
from jax.experimental import pallas as pl
from jax.experimental.pallas import tpu as pltpu
from jax.sharding import PartitionSpec as P

HD = 64
WINDOW = 512
NG = 2
ROWS_DEV = 2048
SLOTS = 5
EPS = 1e-06
NEG = -1e30
AXES = ("seq", "table")
LANES = 128
BF16 = jnp.bfloat16
F32 = jnp.float32
I32 = jnp.int32
GROUPS = (4, 2)


def iota(shape, dim):
    return lax.broadcasted_iota(I32, shape, dim)


def dot(left, right, left_dim, right_dim):
    return lax.dot_general(
        left, right, (((left_dim,), (right_dim,)), ((), ())), preferred_element_type=F32
    )


def params(mib):
    return pltpu.CompilerParams(vmem_limit_bytes=mib * 1024 * 1024)


def shifted(shard, by):
    count = lax.axis_size(AXES)
    pairs = [(i, i + by) for i in range(count) if 0 <= i + by < count]
    return lax.ppermute(shard, AXES, pairs)


MAIN = 4
CHUNK = 64


def slots_kernel(first_ref, row_ref, col_ref, slot_ref, label_ref):
    count = row_ref.shape[1]
    places = label_ref.shape[1]
    odd = lax.rem(first_ref[0] // count, 2)
    labels = jnp.full((1, places), ROWS_DEV, I32)
    sub = iota((count, count), 0)
    lane = iota((count, count), 1)
    for table in range(NG):
        row = row_ref[table : table + 1, :]
        col = col_ref[:, table : table + 1]
        same = col == row
        first_col = jnp.sum((same & (lane < sub)).astype(I32), axis=1, keepdims=True) == 0
        first_row = jnp.sum((same & (sub < lane)).astype(I32), axis=0, keepdims=True) == 0
        row_owner = row // ROWS_DEV
        col_owner = col // ROWS_DEV
        mates = row_owner == col_owner
        place_row = jnp.sum((first_col & mates & (col < row)).astype(I32), axis=0, keepdims=True)
        place_col = jnp.sum((first_row & mates & (row < col)).astype(I32), axis=1, keepdims=True)
        side = lax.rem(table + odd, 2)
        main = row_owner * (NG * MAIN) + side * MAIN + place_row
        slot_ref[table : table + 1, :] = jnp.where(place_row < MAIN, main, -1)
        last = row_owner * NG + table
        slot_ref[NG + table : NG + table + 1, :] = jnp.where(place_row < MAIN, -1, last)
        slot_col = col_owner * (NG * SLOTS) + table * SLOTS + place_col
        local_col = col - col_owner * ROWS_DEV
        hit = slot_col == iota((count, places), 1)
        labels = jnp.minimum(
            labels, jnp.min(jnp.where(hit, local_col, ROWS_DEV), axis=0, keepdims=True)
        )
    label_ref[...] = labels


def make_slots(first, hash_ids, devices):
    count = hash_ids.shape[1]
    places = devices * NG * SLOTS
    return pl.pallas_call(
        slots_kernel,
        in_specs=[
            pl.BlockSpec(memory_space=pltpu.SMEM),
            pl.BlockSpec(memory_space=pltpu.VMEM),
            pl.BlockSpec(memory_space=pltpu.VMEM),
        ],
        out_shape=(
            jax.ShapeDtypeStruct((2 * NG, count), I32),
            jax.ShapeDtypeStruct((1, places), I32),
        ),
        compiler_params=params(56),
        name="slots",
    )(first, hash_ids, jnp.transpose(hash_ids))


QT = 256
KT = QT + WINDOW


def attention_kernel(
    first_ref, len_ref, q_ref, kp_ref, ko_ref, vp_ref, vo_ref, da_ref,
    dq_ref, back_ref, dko_ref, dvo_ref,
    bias_ref, kx_ref, vx_ref, dk_ref, dv_ref,
):
    count = q_ref.shape[0]
    tiles = count // QT

    @pl.when(pl.program_id(0) == 0)
    def _():
        docs = len_ref.shape[1]
        first = first_ref[0]
        upto = iota((docs, docs), 1) <= iota((docs, docs), 0)
        ends = jnp.sum(jnp.where(upto, len_ref[...], 0), axis=1, keepdims=True)
        qpos = first + iota((1, count), 1)
        start = jnp.max(jnp.where(ends <= qpos, ends, 0), axis=0, keepdims=True)
        low = jnp.maximum(start, qpos - (WINDOW - 1))
        for tile in range(tiles):
            cols = slice(tile * QT, (tile + 1) * QT)
            kpos = first - WINDOW + tile * QT + iota((KT, QT), 0)
            ok = (kpos >= low[:, cols]) & (kpos <= qpos[:, cols])
            bias_ref[tile] = jnp.where(ok, 0.0, NEG)

    kx_ref[:WINDOW] = kp_ref[0]
    kx_ref[WINDOW:] = ko_ref[...]
    vx_ref[:WINDOW] = vp_ref[0]
    vx_ref[WINDOW:] = vo_ref[...]
    lane = iota((QT, LANES), 1)
    scale = HD ** (-0.5)
    zero = jnp.zeros((QT, LANES), BF16)
    steps = [(tile, half) for tile in range(tiles) for half in range(LANES // HD)]
    rowlane = iota((LANES, QT), 0)

    def open_step(step):
        tile, half = step
        rows = slice(tile * QT, (tile + 1) * QT)
        span = slice(tile * QT, tile * QT + KT)
        mine = (lane // HD) == half
        qh = jnp.where(mine, q_ref[rows, :] * jnp.asarray(scale, BF16), zero)
        dah = jnp.where(mine, da_ref[rows, :], zero)
        score = dot(kx_ref[span, :], qh, 1, 1) + bias_ref[tile]
        dprob = dot(vx_ref[span, :], dah, 1, 1)
        return qh, dah, score, dprob

    def soften(opened):
        qh, dah, score, dprob = opened
        top = jnp.max(score, axis=0, keepdims=True)
        expo = jnp.exp(score - top)
        total = jnp.sum(expo, axis=0, keepdims=True)
        prob = expo * (1.0 / total)
        both = prob * dprob
        delta = jnp.sum(both, axis=0, keepdims=True)
        return qh, dah, prob.astype(BF16), (both - prob * delta).astype(BF16)

    def close(tile, first_half, second_half):
        rows = slice(tile * QT, (tile + 1) * QT)
        span = slice(tile * QT, tile * QT + KT)
        q0, da0, p0, s0 = first_half
        q1, da1, p1, s1 = second_half
        joined = lambda x, y, axis: jnp.concatenate([x, y], axis=axis)
        dv = dot(joined(p0, p1, 1), joined(da0, da1, 0), 1, 0)
        ds = joined(s0, s1, 1)
        dk = dot(ds, joined(q0, q1, 0), 1, 0)
        dq = dot(kx_ref[span, :], ds, 0, 0)
        dq = jnp.where(rowlane < HD, dq[:, :QT], dq[:, QT:])
        dq_ref[rows, :] = jnp.transpose(dq * scale).astype(BF16)
        if tile == 0:
            dk_ref[span, :] = dk
            dv_ref[span, :] = dv
        else:
            seen = slice(tile * QT, (tile - 1) * QT + KT)
            fresh = slice((tile - 1) * QT + KT, tile * QT + KT)
            both = KT - QT
            dk_ref[seen, :] += dk[:both]
            dv_ref[seen, :] += dv[:both]
            dk_ref[fresh, :] = dk[both:]
            dv_ref[fresh, :] = dv[both:]

    opened = open_step(steps[0])
    soft = []
    for n, (tile, half) in enumerate(steps):
        later = open_step(steps[n + 1]) if n + 1 < len(steps) else None
        soft.append(soften(opened))
        opened = later
        if half == 1:
            close(tile, soft[-2], soft[-1])
    pass
    back_ref[0] = dk_ref[:WINDOW].astype(BF16)
    back_ref[1] = dv_ref[:WINDOW].astype(BF16)
    dko_ref[...] = dk_ref[WINDOW:]
    dvo_ref[...] = dv_ref[WINDOW:]


def attention_grads(first, doc_lengths, queries, halo, keys, values, grad_attn, at):
    count = queries.shape[0]
    width = halo.shape[2]
    pairs = width // LANES
    ext = count + WINDOW
    tiles = count // QT
    column = pl.BlockSpec((count, LANES), lambda i: (0, i + at))
    fresh = pl.BlockSpec((count, LANES), lambda i: (0, i))
    docs = doc_lengths.shape[0]
    return pl.pallas_call(
        attention_kernel,
        grid=(pairs,),
        in_specs=[
            pl.BlockSpec(memory_space=pltpu.SMEM),
            pl.BlockSpec((1, docs), lambda i: (0, 0)),
            column,
            pl.BlockSpec((1, WINDOW, LANES), lambda i: (0, 0, i)),
            column,
            pl.BlockSpec((1, WINDOW, LANES), lambda i: (1, 0, i)),
            column,
            column,
        ],
        out_specs=[fresh, pl.BlockSpec((2, WINDOW, LANES), lambda i: (0, 0, i)), fresh, fresh],
        out_shape=[
            jax.ShapeDtypeStruct((count, width), BF16),
            jax.ShapeDtypeStruct((2, WINDOW, width), BF16),
            jax.ShapeDtypeStruct((count, width), F32),
            jax.ShapeDtypeStruct((count, width), F32),
        ],
        scratch_shapes=[
            pltpu.VMEM((tiles, KT, QT), F32),
            pltpu.VMEM((ext, LANES), BF16),
            pltpu.VMEM((ext, LANES), BF16),
            pltpu.VMEM((ext, LANES), F32),
            pltpu.VMEM((ext, LANES), F32),
        ],
        compiler_params=params(56),
        cost_estimate=pl.CostEstimate(
            flops=10 * count * KT * width, bytes_accessed=20 * count * width,
            transcendentals=count * KT * width // HD,
        ),
        name="attention",
    )(first, doc_lengths.reshape(1, docs), queries, halo, keys, halo, values, grad_attn)


PACK = 32
SPREAD = 16


def finish_kernel(*refs):
    groups = len(GROUPS)
    parts = [refs[4 * g : 4 * g + 4] for g in range(groups)]
    (
        wq_in, wk_in, wv_in, hidden_in, out_in, gain_ref, slot_ref, gh_out, sent_out,
        dq_ref, dk_ref, dv_ref, back_ref, wq_ref, wk_ref, wv_ref, hidden_ref, out_ref,
        gh_ref, sent_ref, sems,
    ) = refs[4 * groups :]
    count, width = hidden_ref.shape
    devices = sent_ref.shape[0]
    started = []

    def bring(*pairs):
        copies = []
        for source, target in pairs:
            copies.append(pltpu.make_async_copy(source, target, sems.at[len(started)]))
            started.append(copies[-1])
            copies[-1].start()
        return copies

    def arrive(copies):
        for copy in copies:
            copy.wait()

    spans = []
    at = 0
    for pairs in GROUPS:
        spans.append(slice(at * LANES, (at + pairs) * LANES))
        at += pairs
    need_hidden = bring((hidden_in, hidden_ref))
    need_q = bring(*[(p[0], dq_ref.at[:, c]) for p, c in zip(parts, spans)], (wq_in, wq_ref))
    need_k = bring(
        *[(p[1].at[0], back_ref.at[0, :, c]) for p, c in zip(parts, spans)],
        *[(p[2], dk_ref.at[:, c]) for p, c in zip(parts, spans)],
        (wk_in, wk_ref),
    )
    need_v = bring(
        *[(p[1].at[1], back_ref.at[1, :, c]) for p, c in zip(parts, spans)],
        *[(p[3], dv_ref.at[:, c]) for p, c in zip(parts, spans)],
        (wv_in, wv_ref),
    )
    need_out = bring((out_in, out_ref))

    def hits(place, at):
        hit = place == slot_ref[at : at + 1, :]
        for table in range(1, NG):
            hit = hit | (place == slot_ref[at + table : at + table + 1, :])
        return jnp.where(hit, 1.0, 0.0).astype(BF16)

    blocks = width // LANES
    both = NG * MAIN
    tail = CHUNK - blocks * both
    shape = (SPREAD * tail, blocks * SPREAD * NG)
    row = iota((shape[0], 1), 0)
    inner = lax.rem(row, tail)
    source = (inner // NG) * (SPREAD * NG) + (row // tail) * NG + lax.rem(inner, NG)
    lay = jnp.where((inner < blocks * NG) & (source == iota(shape, 1)), 1.0, 0.0).astype(BF16)

    arrive(need_hidden)
    full = hidden_ref[...].astype(F32)
    inverse = lax.rsqrt(jnp.mean(full * full, axis=1, keepdims=True) + EPS)
    arrive(need_q)
    norm = dot(dq_ref[...], wq_ref[...], 1, 1)
    arrive(need_k)
    norm = norm + dot((dk_ref[...] + back_ref[0].astype(F32)).astype(BF16), wk_ref[...], 1, 1)
    arrive(need_v)
    norm = norm + dot((dv_ref[...] + back_ref[1].astype(F32)).astype(BF16), wv_ref[...], 1, 1)
    arrive(need_out)
    unit = hidden_ref[...].astype(F32) * inverse
    scaled = norm * gain_ref[...]
    through = inverse * (scaled - unit * jnp.mean(scaled * unit, axis=1, keepdims=True))
    grad_hidden = (out_ref[...].astype(F32) + through).astype(BF16)
    gh_ref[...] = grad_hidden
    leaving = bring((gh_ref, gh_out))

    cut = lambda value, c: value[:, c * LANES : (c + 1) * LANES]
    rest = dot(hits(iota((devices * NG, count), 0), NG), grad_hidden, 1, 0).astype(BF16)
    for at in range(0, devices, PACK):
        place = at * both + iota((PACK * both, count), 0)
        main = dot(hits(place, 0), grad_hidden, 1, 0)
        for c in range(0, blocks, 2):
            pair = [cut(main, c + i).reshape(PACK, both, LANES) for i in range(2)]
            sent_ref[at : at + PACK, c * both : (c + 2) * both, :] = jnp.concatenate(
                pair, axis=1
            ).astype(BF16)
        for low in range(at, at + PACK, SPREAD):
            some = rest[low * NG : (low + SPREAD) * NG]
            some = jnp.concatenate([cut(some, c) for c in range(blocks)], axis=0)
            sent_ref[low : low + SPREAD, blocks * both :, :] = (
                dot(lay, some, 1, 0).reshape(SPREAD, tail, LANES).astype(BF16)
            )
        leaving += bring((sent_ref.at[at : at + PACK], sent_out.at[at : at + PACK]))
    arrive(leaving)


def finish(parts, wq, wk, wv, hidden, gain, grad_out, slot, devices):
    count, width = hidden.shape
    groups = len(GROUPS)
    place = pl.BlockSpec(memory_space=pl.ANY)
    small = pl.BlockSpec(memory_space=pltpu.VMEM)
    copies = 5 * groups + 6 + devices // PACK
    return pl.pallas_call(
        finish_kernel,
        in_specs=[place] * (4 * groups + 5) + [small] * 2,
        out_specs=(place, place),
        out_shape=(
            jax.ShapeDtypeStruct((count, width), BF16),
            jax.ShapeDtypeStruct((devices, CHUNK, LANES), BF16),
        ),
        scratch_shapes=[
            pltpu.VMEM((count, width), BF16),
            pltpu.VMEM((count, width), F32),
            pltpu.VMEM((count, width), F32),
            pltpu.VMEM((2, WINDOW, width), BF16),
            pltpu.VMEM((width, width), BF16),
            pltpu.VMEM((width, width), BF16),
            pltpu.VMEM((width, width), BF16),
            pltpu.VMEM((count, width), BF16),
            pltpu.VMEM((count, width), BF16),
            pltpu.VMEM((count, width), BF16),
            pltpu.VMEM((devices, CHUNK, LANES), BF16),
            pltpu.SemaphoreType.DMA((copies,)),
        ],
        compiler_params=params(56),
        name="finish",
    )(
        *[array for part in parts for array in part],
        wq, wk, wv, hidden, grad_out, gain.reshape(1, width), slot,
    )


COLLECT = 1024
APART = 16


def collect_kernel(label_ref, got_ref, out_ref, rows_ref):
    devices = got_ref.shape[0]
    blocks = rows_ref.shape[2] // LANES
    both = NG * MAIN
    tail = CHUNK - blocks * both
    mains = devices * MAIN

    @pl.when((pl.program_id(0) == 0) & (pl.program_id(1) == 0))
    def _():
        low = iota((devices // 2, both, LANES), 1) < MAIN
        for c in range(0, blocks, 2):
            wide = got_ref[:, c * both : (c + 2) * both, :].astype(F32)
            for i in range(2):
                cols = slice((c + i) * LANES, (c + i + 1) * LANES)
                piece = wide[:, i * both : (i + 1) * both, :]
                piece = piece.reshape(devices // 2, 2, both, LANES)
                even, odd = piece[:, 0], piece[:, 1]
                zero = jnp.where(low, even, odd).reshape(mains, LANES)
                one = jnp.where(low, odd, even).reshape(mains, LANES)
                rows_ref[0, :mains, cols] = zero.astype(BF16)
                rows_ref[1, :mains, cols] = one.astype(BF16)
        shape = (NG * blocks * APART, APART * tail)
        row = iota((shape[0], 1), 0)
        device = lax.rem(row, APART)
        block = lax.rem(row // APART, blocks)
        table = row // (APART * blocks)
        source = device * tail + block * NG + table
        pick = jnp.where(source == iota(shape, 1), 1.0, 0.0).astype(BF16)
        for at in range(0, devices, APART):
            rest = got_ref[at : at + APART, blocks * both :, :].reshape(APART * tail, LANES)
            rest = dot(pick, rest, 1, 0).astype(BF16)
            for t in range(NG):
                for c in range(blocks):
                    start = (t * blocks + c) * APART
                    rows_ref[t, mains + at : mains + at + APART, c * LANES : (c + 1) * LANES] = rest[
                        start : start + APART
                    ]

    place = pl.program_id(1) * COLLECT + iota((COLLECT, label_ref.shape[2]), 0)
    hit = jnp.where(place == label_ref[0], 1.0, 0.0).astype(BF16)
    out_ref[0] = dot(hit, rows_ref[pl.program_id(0)], 1, 0).astype(BF16)


def collect(labels, got, width):
    tables, _, number = labels.shape
    return pl.pallas_call(
        collect_kernel,
        grid=(tables, ROWS_DEV // COLLECT),
        in_specs=[
            pl.BlockSpec((1, 1, number), lambda t, i: (t, 0, 0)),
            pl.BlockSpec(got.shape, lambda t, i: (0, 0, 0)),
        ],
        out_specs=pl.BlockSpec((1, COLLECT, width), lambda t, i: (t, i, 0)),
        out_shape=jax.ShapeDtypeStruct((tables, ROWS_DEV, width), BF16),
        scratch_shapes=[pltpu.VMEM((tables, number, width), BF16)],
        compiler_params=params(28),
        name="collect",
    )(labels, got)


def exchanged(part):
    return lax.all_to_all(part, AXES, split_axis=0, concat_axis=0, tiled=True)


def shards(
    hidden,
    gain,
    queries,
    keys,
    values,
    w_query,
    w_key,
    w_value,
    w_out,
    grad_out,
    doc_lengths,
    hash_ids,
):
    count, width = hidden.shape
    devices = lax.axis_size(AXES)
    first = (lax.axis_index(AXES) * count).astype(I32).reshape(1)
    halos = []
    at = 0
    for pairs in GROUPS:
        cols = slice(at * LANES, (at + pairs) * LANES)
        halos.append(shifted(jnp.stack([keys[:, cols], values[:, cols]]), 1))
        at += pairs
    grad_attn = dot(grad_out, w_out, 1, 1).astype(BF16)
    slot, labels = make_slots(first, hash_ids, devices)
    grad_attn, slot, labels = lax.optimization_barrier((grad_attn, slot, labels))
    parts = []
    at = 0
    for pairs, halo in zip(GROUPS, halos):
        dq, back, dk, dv = attention_grads(
            first, doc_lengths, queries, halo, keys, values, grad_attn, at
        )
        parts.append((dq, shifted(back, -1), dk, dv))
        at += pairs
    labels, _ = lax.optimization_barrier((labels, parts[-1][0]))
    labels = exchanged(labels.reshape(devices, NG, SLOTS))
    labels = jnp.transpose(labels, (1, 0, 2))
    main = labels[:, :, :MAIN].reshape(NG, devices // 2, 2, MAIN)
    main = jnp.stack([main[0], main[1, :, ::-1]])
    labels = jnp.concatenate([main.reshape(NG, devices * MAIN), labels[:, :, MAIN]], axis=1)
    grad_hidden, sent = finish(
        parts, w_query, w_key, w_value, hidden, gain, grad_out, slot, devices
    )
    return grad_hidden, collect(labels[:, None, :], exchanged(sent), width)


def solution(mesh):
    spread = P(AXES, None)
    return jax.shard_map(
        shards,
        mesh=mesh,
        in_specs=(
            spread, P(), spread, spread, spread, P(), P(), P(), P(), spread, P(), P(None, AXES),
        ),
        out_specs=(spread, P(None, AXES, None)),
        check_vma=False,
    )
```

```python
import functools

import jax
import jax.numpy as jnp
from jax import lax
from jax.experimental import pallas as pl
from jax.experimental.pallas import tpu as pltpu
from jax.sharding import PartitionSpec as P

HD = 64
WINDOW = 512
NG = 2
ROWS_DEV = 2048
SLOTS = 5
EPS = 1e-06
NEG = -1e30
AXES = ("seq", "table")
LANES = 128
BF16 = jnp.bfloat16
F32 = jnp.float32
I32 = jnp.int32
GROUPS = (3, 3)


def iota(shape, dim):
    return lax.broadcasted_iota(I32, shape, dim)


def dot(left, right, left_dim, right_dim):
    return lax.dot_general(
        left, right, (((left_dim,), (right_dim,)), ((), ())), preferred_element_type=F32
    )


def params(mib):
    return pltpu.CompilerParams(vmem_limit_bytes=mib * 1024 * 1024)


def shifted(shard, by):
    count = lax.axis_size(AXES)
    pairs = [(i, i + by) for i in range(count) if 0 <= i + by < count]
    return lax.ppermute(shard, AXES, pairs)


MAIN = 4
CHUNK = 64
MARK = 64


def slots_kernel(first_ref, row_ref, col_ref, slot_ref, mark_ref):
    count = row_ref.shape[1]
    devices = mark_ref.shape[1]
    odd = lax.rem(first_ref[0] // count, 2)
    high = low = jnp.zeros((devices, LANES), F32)
    sub = iota((count, count), 0)
    lane = iota((count, count), 1)
    for table in range(NG):
        row = row_ref[table : table + 1, :]
        col = col_ref[:, table : table + 1]
        same = col == row
        first_col = jnp.sum((same & (lane < sub)).astype(I32), axis=1, keepdims=True) == 0
        first_row = jnp.sum((same & (sub < lane)).astype(I32), axis=0, keepdims=True) == 0
        row_owner = row // ROWS_DEV
        col_owner = col // ROWS_DEV
        mates = row_owner == col_owner
        place_row = jnp.sum((first_col & mates & (col < row)).astype(I32), axis=0, keepdims=True)
        place_col = jnp.sum((first_row & mates & (row < col)).astype(I32), axis=1, keepdims=True)
        side = lax.rem(table + odd, 2)
        main = row_owner * (NG * MAIN) + side * MAIN + place_row
        slot_ref[table : table + 1, :] = jnp.where(place_row < MAIN, main, -1)
        last = row_owner * NG + table
        slot_ref[NG + table : NG + table + 1, :] = jnp.where(place_row < MAIN, -1, last)
        value = col - col_owner * ROWS_DEV + 1
        here = first_col & (iota((count, LANES), 1) == table * SLOTS + place_col)
        owned = jnp.where(row_owner == iota((devices, count), 0), 1.0, 0.0).astype(BF16)
        part = lambda x: jnp.where(here, x.astype(F32), 0.0).astype(BF16)
        high = high + dot(owned, part(value // MARK), 1, 0)
        low = low + dot(owned, part(lax.rem(value, MARK)), 1, 0)
    mark_ref[0] = high.astype(BF16)
    mark_ref[1] = low.astype(BF16)


def make_slots(first, hash_ids, devices):
    count = hash_ids.shape[1]
    return pl.pallas_call(
        slots_kernel,
        in_specs=[
            pl.BlockSpec(memory_space=pltpu.SMEM),
            pl.BlockSpec(memory_space=pltpu.VMEM),
            pl.BlockSpec(memory_space=pltpu.VMEM),
        ],
        out_shape=(
            jax.ShapeDtypeStruct((2 * NG, count), I32),
            jax.ShapeDtypeStruct((2, devices, LANES), BF16),
        ),
        compiler_params=params(56),
        name="slots",
    )(first, hash_ids, jnp.transpose(hash_ids))


QT = 256
KT = QT + WINDOW


def attention_kernel(
    first_ref, len_ref, q_ref, kp_ref, ko_ref, vp_ref, vo_ref, da_ref,
    dq_ref, back_ref, dko_ref, dvo_ref,
    bias_ref, kx_ref, vx_ref, dk_ref, dv_ref,
):
    count = q_ref.shape[0]
    tiles = count // QT

    @pl.when(pl.program_id(0) == 0)
    def _():
        docs = len_ref.shape[1]
        first = first_ref[0]
        upto = iota((docs, docs), 1) <= iota((docs, docs), 0)
        ends = jnp.sum(jnp.where(upto, len_ref[...], 0), axis=1, keepdims=True)
        qpos = first + iota((1, count), 1)
        start = jnp.max(jnp.where(ends <= qpos, ends, 0), axis=0, keepdims=True)
        low = jnp.maximum(start, qpos - (WINDOW - 1))
        for tile in range(tiles):
            cols = slice(tile * QT, (tile + 1) * QT)
            kpos = first - WINDOW + tile * QT + iota((KT, QT), 0)
            ok = (kpos >= low[:, cols]) & (kpos <= qpos[:, cols])
            bias_ref[tile] = jnp.where(ok, 0.0, NEG)

    kx_ref[:WINDOW] = kp_ref[0]
    kx_ref[WINDOW:] = ko_ref[...]
    vx_ref[:WINDOW] = vp_ref[0]
    vx_ref[WINDOW:] = vo_ref[...]
    lane = iota((QT, LANES), 1)
    scale = HD ** (-0.5)
    zero = jnp.zeros((QT, LANES), BF16)
    steps = [(tile, half) for tile in range(tiles) for half in range(LANES // HD)]
    rowlane = iota((LANES, QT), 0)

    def open_step(step):
        tile, half = step
        rows = slice(tile * QT, (tile + 1) * QT)
        span = slice(tile * QT, tile * QT + KT)
        mine = (lane // HD) == half
        qh = jnp.where(mine, q_ref[rows, :] * jnp.asarray(scale, BF16), zero)
        dah = jnp.where(mine, da_ref[rows, :], zero)
        score = dot(kx_ref[span, :], qh, 1, 1) + bias_ref[tile]
        dprob = dot(vx_ref[span, :], dah, 1, 1)
        return qh, dah, score, dprob

    def soften(opened):
        qh, dah, score, dprob = opened
        top = jnp.max(score, axis=0, keepdims=True)
        expo = jnp.exp(score - top)
        total = jnp.sum(expo, axis=0, keepdims=True)
        prob = expo * (1.0 / total)
        both = prob * dprob
        delta = jnp.sum(both, axis=0, keepdims=True)
        return qh, dah, prob.astype(BF16), (both - prob * delta).astype(BF16)

    def close(tile, first_half, second_half):
        rows = slice(tile * QT, (tile + 1) * QT)
        span = slice(tile * QT, tile * QT + KT)
        q0, da0, p0, s0 = first_half
        q1, da1, p1, s1 = second_half
        joined = lambda x, y, axis: jnp.concatenate([x, y], axis=axis)
        dv = dot(joined(p0, p1, 1), joined(da0, da1, 0), 1, 0)
        ds = joined(s0, s1, 1)
        dk = dot(ds, joined(q0, q1, 0), 1, 0)
        dq = dot(kx_ref[span, :], ds, 0, 0)
        dq = jnp.where(rowlane < HD, dq[:, :QT], dq[:, QT:])
        dq_ref[rows, :] = jnp.transpose(dq * scale).astype(BF16)
        if tile == 0:
            dk_ref[span, :] = dk
            dv_ref[span, :] = dv
        else:
            seen = slice(tile * QT, (tile - 1) * QT + KT)
            fresh = slice((tile - 1) * QT + KT, tile * QT + KT)
            both = KT - QT
            dk_ref[seen, :] += dk[:both]
            dv_ref[seen, :] += dv[:both]
            dk_ref[fresh, :] = dk[both:]
            dv_ref[fresh, :] = dv[both:]

    opened = open_step(steps[0])
    soft = []
    for n, (tile, half) in enumerate(steps):
        later = open_step(steps[n + 1]) if n + 1 < len(steps) else None
        soft.append(soften(opened))
        opened = later
        if half == 1:
            close(tile, soft[-2], soft[-1])
    pass
    back_ref[0] = dk_ref[:WINDOW].astype(BF16)
    back_ref[1] = dv_ref[:WINDOW].astype(BF16)
    dko_ref[...] = dk_ref[WINDOW:]
    dvo_ref[...] = dv_ref[WINDOW:]


def attention_grads(first, doc_lengths, queries, halo, keys, values, grad_attn, at):
    count = queries.shape[0]
    width = halo.shape[2]
    pairs = width // LANES
    ext = count + WINDOW
    tiles = count // QT
    column = pl.BlockSpec((count, LANES), lambda i: (0, i + at))
    fresh = pl.BlockSpec((count, LANES), lambda i: (0, i))
    docs = doc_lengths.shape[0]
    return pl.pallas_call(
        attention_kernel,
        grid=(pairs,),
        in_specs=[
            pl.BlockSpec(memory_space=pltpu.SMEM),
            pl.BlockSpec((1, docs), lambda i: (0, 0)),
            column,
            pl.BlockSpec((1, WINDOW, LANES), lambda i: (0, 0, i)),
            column,
            pl.BlockSpec((1, WINDOW, LANES), lambda i: (1, 0, i)),
            column,
            column,
        ],
        out_specs=[fresh, pl.BlockSpec((2, WINDOW, LANES), lambda i: (0, 0, i)), fresh, fresh],
        out_shape=[
            jax.ShapeDtypeStruct((count, width), BF16),
            jax.ShapeDtypeStruct((2, WINDOW, width), BF16),
            jax.ShapeDtypeStruct((count, width), F32),
            jax.ShapeDtypeStruct((count, width), F32),
        ],
        scratch_shapes=[
            pltpu.VMEM((tiles, KT, QT), F32),
            pltpu.VMEM((ext, LANES), BF16),
            pltpu.VMEM((ext, LANES), BF16),
            pltpu.VMEM((ext, LANES), F32),
            pltpu.VMEM((ext, LANES), F32),
        ],
        compiler_params=params(56),
        cost_estimate=pl.CostEstimate(
            flops=10 * count * KT * width, bytes_accessed=20 * count * width,
            transcendentals=count * KT * width // HD,
        ),
        name="attention",
    )(first, doc_lengths.reshape(1, docs), queries, halo, keys, halo, values, grad_attn)


PACK = 32
SPREAD = 16


def finish_kernel(*refs):
    groups = len(GROUPS)
    parts = [refs[3 * g : 3 * g + 3] for g in range(groups)]
    (
        norm_in, wk_in, wv_in, hidden_in, out_in, gain_ref, slot_ref, mark_ref, gh_out, sent_out,
        norm_ref, dk_ref, dv_ref, back_ref, wk_ref, wv_ref, hidden_ref, out_ref,
        gh_ref, sent_ref, sems,
    ) = refs[3 * groups :]
    count, width = hidden_ref.shape
    devices = sent_ref.shape[0]
    started = []

    def bring(*pairs):
        copies = []
        for source, target in pairs:
            copies.append(pltpu.make_async_copy(source, target, sems.at[len(started)]))
            started.append(copies[-1])
            copies[-1].start()
        return copies

    def arrive(copies):
        for copy in copies:
            copy.wait()

    spans = []
    at = 0
    for pairs in GROUPS:
        spans.append(slice(at * LANES, (at + pairs) * LANES))
        at += pairs
    need_hidden = bring((hidden_in, hidden_ref))
    need_k = bring(
        *[(p[0].at[0], back_ref.at[0, :, c]) for p, c in zip(parts, spans)],
        *[(p[1], dk_ref.at[:, c]) for p, c in zip(parts, spans)],
        (wk_in, wk_ref),
    )
    need_norm = bring((norm_in, norm_ref))
    need_v = bring(
        *[(p[0].at[1], back_ref.at[1, :, c]) for p, c in zip(parts, spans)],
        *[(p[2], dv_ref.at[:, c]) for p, c in zip(parts, spans)],
        (wv_in, wv_ref),
    )
    need_out = bring((out_in, out_ref))

    def hits(place, at):
        hit = place == slot_ref[at : at + 1, :]
        for table in range(1, NG):
            hit = hit | (place == slot_ref[at + table : at + table + 1, :])
        return jnp.where(hit, 1.0, 0.0).astype(BF16)

    blocks = width // LANES
    both = NG * MAIN
    tail = CHUNK - blocks * both
    lasts = blocks * NG
    shape = (SPREAD * tail, (lasts + 2) * SPREAD)
    row = iota((shape[0], 1), 0)
    inner = lax.rem(row, tail)
    owner = row // tail
    source = jnp.where(
        inner < lasts,
        (inner // NG) * (SPREAD * NG) + owner * NG + lax.rem(inner, NG),
        inner * SPREAD + owner,
    )
    lay = jnp.where((inner < lasts + 2) & (source == iota(shape, 1)), 1.0, 0.0).astype(BF16)

    arrive(need_hidden)
    full = hidden_ref[...].astype(F32)
    inverse = lax.rsqrt(jnp.mean(full * full, axis=1, keepdims=True) + EPS)
    arrive(need_k)
    norm = dot((dk_ref[...] + back_ref[0].astype(F32)).astype(BF16), wk_ref[...], 1, 1)
    arrive(need_norm)
    norm = norm_ref[...] + norm
    arrive(need_v)
    norm = norm + dot((dv_ref[...] + back_ref[1].astype(F32)).astype(BF16), wv_ref[...], 1, 1)
    arrive(need_out)
    unit = hidden_ref[...].astype(F32) * inverse
    scaled = norm * gain_ref[...]
    through = inverse * (scaled - unit * jnp.mean(scaled * unit, axis=1, keepdims=True))
    grad_hidden = (out_ref[...].astype(F32) + through).astype(BF16)
    gh_ref[...] = grad_hidden
    leaving = bring((gh_ref, gh_out))

    cut = lambda value, c: value[:, c * LANES : (c + 1) * LANES]
    rest = dot(hits(iota((devices * NG, count), 0), NG), grad_hidden, 1, 0).astype(BF16)
    for at in range(0, devices, PACK):
        place = at * both + iota((PACK * both, count), 0)
        main = dot(hits(place, 0), grad_hidden, 1, 0)
        for c in range(0, blocks, 2):
            pair = [cut(main, c + i).reshape(PACK, both, LANES) for i in range(2)]
            sent_ref[at : at + PACK, c * both : (c + 2) * both, :] = jnp.concatenate(
                pair, axis=1
            ).astype(BF16)
        for low in range(at, at + PACK, SPREAD):
            some = rest[low * NG : (low + SPREAD) * NG]
            some = jnp.concatenate(
                [cut(some, c) for c in range(blocks)]
                + [mark_ref[part, low : low + SPREAD, :] for part in range(2)],
                axis=0,
            )
            sent_ref[low : low + SPREAD, blocks * both :, :] = (
                dot(lay, some, 1, 0).reshape(SPREAD, tail, LANES).astype(BF16)
            )
        leaving += bring((sent_ref.at[at : at + PACK], sent_out.at[at : at + PACK]))
    arrive(leaving)


def finish(parts, norm, wk, wv, hidden, gain, grad_out, slot, mark):
    count, width = hidden.shape
    devices = mark.shape[1]
    groups = len(GROUPS)
    place = pl.BlockSpec(memory_space=pl.ANY)
    small = pl.BlockSpec(memory_space=pltpu.VMEM)
    copies = 4 * groups + 6 + devices // PACK
    return pl.pallas_call(
        finish_kernel,
        in_specs=[place] * (3 * groups + 5) + [small] * 3,
        out_specs=(place, place),
        out_shape=(
            jax.ShapeDtypeStruct((count, width), BF16),
            jax.ShapeDtypeStruct((devices, CHUNK, LANES), BF16),
        ),
        scratch_shapes=[
            pltpu.VMEM((count, width), F32),
            pltpu.VMEM((count, width), F32),
            pltpu.VMEM((count, width), F32),
            pltpu.VMEM((2, WINDOW, width), BF16),
            pltpu.VMEM((width, width), BF16),
            pltpu.VMEM((width, width), BF16),
            pltpu.VMEM((count, width), BF16),
            pltpu.VMEM((count, width), BF16),
            pltpu.VMEM((count, width), BF16),
            pltpu.VMEM((devices, CHUNK, LANES), BF16),
            pltpu.SemaphoreType.DMA((copies,)),
        ],
        compiler_params=params(56),
        name="finish",
    )(
        *[array for part in parts for array in part],
        norm, wk, wv, hidden, grad_out, gain.reshape(1, width), slot, mark,
    )


COLLECT = 1024
APART = 16


def collect_kernel(got_ref, out_ref, rows_ref, mark_ref, label_ref):
    devices = got_ref.shape[0]
    blocks = rows_ref.shape[2] // LANES
    both = NG * MAIN
    tail = CHUNK - blocks * both
    mains = devices * MAIN

    @pl.when((pl.program_id(0) == 0) & (pl.program_id(1) == 0))
    def _():
        low = iota((devices // 2, both, LANES), 1) < MAIN
        for c in range(0, blocks, 2):
            wide = got_ref[:, c * both : (c + 2) * both, :].astype(F32)
            for i in range(2):
                cols = slice((c + i) * LANES, (c + i + 1) * LANES)
                piece = wide[:, i * both : (i + 1) * both, :]
                piece = piece.reshape(devices // 2, 2, both, LANES)
                even, odd = piece[:, 0], piece[:, 1]
                zero = jnp.where(low, even, odd).reshape(mains, LANES)
                one = jnp.where(low, odd, even).reshape(mains, LANES)
                rows_ref[0, :mains, cols] = zero.astype(BF16)
                rows_ref[1, :mains, cols] = one.astype(BF16)
        lasts = NG * blocks
        shape = ((lasts + 2) * APART, APART * tail)
        row = iota((shape[0], 1), 0)
        device = lax.rem(row, APART)
        block = lax.rem(row // APART, blocks)
        table = row // (APART * blocks)
        source = device * tail + jnp.where(table < NG, block * NG + table, row // APART)
        pick = jnp.where(source == iota(shape, 1), 1.0, 0.0).astype(BF16)
        for at in range(0, devices, APART):
            rest = got_ref[at : at + APART, blocks * both :, :].reshape(APART * tail, LANES)
            rest = dot(pick, rest, 1, 0).astype(BF16)
            for t in range(NG):
                for c in range(blocks):
                    start = (t * blocks + c) * APART
                    rows_ref[t, mains + at : mains + at + APART, c * LANES : (c + 1) * LANES] = rest[
                        start : start + APART
                    ]
            for part in range(2):
                start = (lasts + part) * APART
                mark_ref[part, at : at + APART, :] = rest[start : start + APART]
        number = label_ref.shape[2]
        k = iota((1, number), 1)
        for t in range(NG):
            source = k // MAIN
            if t == 1:
                source = source + 1 - 2 * lax.rem(source, 2)
            source = jnp.where(k < mains, source, k - mains)
            slot = t * SLOTS + jnp.where(k < mains, lax.rem(k, MAIN), MAIN)
            take = jnp.where(slot == iota((LANES, number), 0), 1.0, 0.0).astype(BF16)
            value = MARK * dot(mark_ref[0], take, 1, 0) + dot(mark_ref[1], take, 1, 0)
            value = jnp.where(source == iota((devices, number), 0), value, 0.0)
            label_ref[t] = jnp.sum(value, axis=0, keepdims=True).astype(I32) - 1

    place = pl.program_id(1) * COLLECT + iota((COLLECT, label_ref.shape[2]), 0)
    hit = jnp.where(place == label_ref[pl.program_id(0)], 1.0, 0.0).astype(BF16)
    out_ref[0] = dot(hit, rows_ref[pl.program_id(0)], 1, 0).astype(BF16)


def collect(got, width):
    devices = got.shape[0]
    number = devices * SLOTS
    return pl.pallas_call(
        collect_kernel,
        grid=(NG, ROWS_DEV // COLLECT),
        in_specs=[pl.BlockSpec(got.shape, lambda t, i: (0, 0, 0))],
        out_specs=pl.BlockSpec((1, COLLECT, width), lambda t, i: (t, i, 0)),
        out_shape=jax.ShapeDtypeStruct((NG, ROWS_DEV, width), BF16),
        scratch_shapes=[
            pltpu.VMEM((NG, number, width), BF16),
            pltpu.VMEM((2, devices, LANES), BF16),
            pltpu.VMEM((NG, 1, number), I32),
        ],
        compiler_params=params(28),
        name="collect",
    )(got)


def exchanged(part):
    return lax.all_to_all(part, AXES, split_axis=0, concat_axis=0, tiled=True)


def shards(
    hidden,
    gain,
    queries,
    keys,
    values,
    w_query,
    w_key,
    w_value,
    w_out,
    grad_out,
    doc_lengths,
    hash_ids,
):
    count, width = hidden.shape
    devices = lax.axis_size(AXES)
    first = (lax.axis_index(AXES) * count).astype(I32).reshape(1)
    halos = []
    at = 0
    for pairs in GROUPS:
        cols = slice(at * LANES, (at + pairs) * LANES)
        halos.append(shifted(jnp.stack([keys[:, cols], values[:, cols]]), 1))
        at += pairs
    grad_attn = dot(grad_out, w_out, 1, 1).astype(BF16)
    slot, mark = make_slots(first, hash_ids, devices)
    grad_attn, slot, mark = lax.optimization_barrier((grad_attn, slot, mark))
    parts = []
    queries_part = []
    at = 0
    for pairs, halo in zip(GROUPS, halos):
        dq, back, dk, dv = attention_grads(
            first, doc_lengths, queries, halo, keys, values, grad_attn, at
        )
        queries_part.append(dq)
        parts.append((shifted(back, -1), dk, dv))
        at += pairs
    grad_q = jnp.concatenate(lax.optimization_barrier(queries_part), axis=1)
    norm = dot(grad_q, w_query, 1, 1)
    grad_hidden, sent = finish(
        parts, norm, w_key, w_value, hidden, gain, grad_out, slot, mark
    )
    return grad_hidden, collect(exchanged(sent), width)


def solution(mesh):
    spread = P(AXES, None)
    return jax.shard_map(
        shards,
        mesh=mesh,
        in_specs=(
            spread, P(), spread, spread, spread, P(), P(), P(), P(), spread, P(), P(None, AXES),
        ),
        out_specs=(spread, P(None, AXES, None)),
        check_vma=False,
    )
```

```python
import functools

import jax
import jax.numpy as jnp
from jax import lax
from jax.experimental import pallas as pl
from jax.experimental.pallas import tpu as pltpu
from jax.sharding import PartitionSpec as P

HD = 64
WINDOW = 512
NG = 2
ROWS_DEV = 2048
SLOTS = 5
EPS = 1e-06
NEG = -1e30
AXES = ("seq", "table")
LANES = 128
BF16 = jnp.bfloat16
F32 = jnp.float32
I32 = jnp.int32
GROUPS = (3, 3)


def iota(shape, dim):
    return lax.broadcasted_iota(I32, shape, dim)


def dot(left, right, left_dim, right_dim):
    return lax.dot_general(
        left, right, (((left_dim,), (right_dim,)), ((), ())), preferred_element_type=F32
    )


def params(mib):
    return pltpu.CompilerParams(vmem_limit_bytes=mib * 1024 * 1024)


def shifted(shard, by):
    count = lax.axis_size(AXES)
    pairs = [(i, i + by) for i in range(count) if 0 <= i + by < count]
    return lax.ppermute(shard, AXES, pairs)


MAIN = 4
CHUNK = 64
MARK = 64


def slots_kernel(first_ref, row_ref, col_ref, slot_ref, mark_ref):
    count = row_ref.shape[1]
    devices = mark_ref.shape[1]
    odd = lax.rem(first_ref[0] // count, 2)
    high = low = jnp.zeros((devices, LANES), F32)
    sub = iota((count, count), 0)
    lane = iota((count, count), 1)
    for table in range(NG):
        row = row_ref[table : table + 1, :]
        col = col_ref[:, table : table + 1]
        same = col == row
        first_col = jnp.sum((same & (lane < sub)).astype(I32), axis=1, keepdims=True) == 0
        first_row = jnp.sum((same & (sub < lane)).astype(I32), axis=0, keepdims=True) == 0
        row_owner = row // ROWS_DEV
        col_owner = col // ROWS_DEV
        mates = row_owner == col_owner
        place_row = jnp.sum((first_col & mates & (col < row)).astype(I32), axis=0, keepdims=True)
        place_col = jnp.sum((first_row & mates & (row < col)).astype(I32), axis=1, keepdims=True)
        side = lax.rem(table + odd, 2)
        main = row_owner * (NG * MAIN) + side * MAIN + place_row
        slot_ref[table : table + 1, :] = jnp.where(place_row < MAIN, main, -1)
        last = row_owner * NG + table
        slot_ref[NG + table : NG + table + 1, :] = jnp.where(place_row < MAIN, -1, last)
        value = col - col_owner * ROWS_DEV + 1
        here = first_col & (iota((count, LANES), 1) == table * SLOTS + place_col)
        owned = jnp.where(row_owner == iota((devices, count), 0), 1.0, 0.0).astype(BF16)
        part = lambda x: jnp.where(here, x.astype(F32), 0.0).astype(BF16)
        high = high + dot(owned, part(value // MARK), 1, 0)
        low = low + dot(owned, part(lax.rem(value, MARK)), 1, 0)
    mark_ref[0] = high.astype(BF16)
    mark_ref[1] = low.astype(BF16)


def make_slots(first, hash_ids, devices):
    count = hash_ids.shape[1]
    return pl.pallas_call(
        slots_kernel,
        in_specs=[
            pl.BlockSpec(memory_space=pltpu.SMEM),
            pl.BlockSpec(memory_space=pltpu.VMEM),
            pl.BlockSpec(memory_space=pltpu.VMEM),
        ],
        out_shape=(
            jax.ShapeDtypeStruct((2 * NG, count), I32),
            jax.ShapeDtypeStruct((2, devices, LANES), BF16),
        ),
        compiler_params=params(56),
        name="slots",
    )(first, hash_ids, jnp.transpose(hash_ids))


QT = 256
KT = QT + WINDOW


def attention_kernel(
    first_ref, len_ref, q_ref, kp_ref, ko_ref, vp_ref, vo_ref, da_ref,
    dq_ref, back_ref, dko_ref, dvo_ref,
    bias_ref, kx_ref, vx_ref, dk_ref, dv_ref,
):
    count = q_ref.shape[0]
    tiles = count // QT

    @pl.when(pl.program_id(0) == 0)
    def _():
        docs = len_ref.shape[1]
        first = first_ref[0]
        upto = iota((docs, docs), 1) <= iota((docs, docs), 0)
        ends = jnp.sum(jnp.where(upto, len_ref[...], 0), axis=1, keepdims=True)
        qpos = first + iota((1, count), 1)
        start = jnp.max(jnp.where(ends <= qpos, ends, 0), axis=0, keepdims=True)
        low = jnp.maximum(start, qpos - (WINDOW - 1))
        for tile in range(tiles):
            cols = slice(tile * QT, (tile + 1) * QT)
            kpos = first - WINDOW + tile * QT + iota((KT, QT), 0)
            ok = (kpos >= low[:, cols]) & (kpos <= qpos[:, cols])
            bias_ref[tile] = jnp.where(ok, 0.0, NEG)

    kx_ref[:WINDOW] = kp_ref[0]
    kx_ref[WINDOW:] = ko_ref[...]
    vx_ref[:WINDOW] = vp_ref[0]
    vx_ref[WINDOW:] = vo_ref[...]
    lane = iota((QT, LANES), 1)
    scale = HD ** (-0.5)
    zero = jnp.zeros((QT, LANES), BF16)
    steps = [(tile, half) for tile in range(tiles) for half in range(LANES // HD)]
    rowlane = iota((LANES, QT), 0)

    def open_step(step):
        tile, half = step
        rows = slice(tile * QT, (tile + 1) * QT)
        span = slice(tile * QT, tile * QT + KT)
        mine = (lane // HD) == half
        qh = jnp.where(mine, q_ref[rows, :] * jnp.asarray(scale, BF16), zero)
        dah = jnp.where(mine, da_ref[rows, :], zero)
        score = dot(kx_ref[span, :], qh, 1, 1) + bias_ref[tile]
        dprob = dot(vx_ref[span, :], dah, 1, 1)
        return qh, dah, score, dprob

    def soften(opened):
        qh, dah, score, dprob = opened
        top = jnp.max(score, axis=0, keepdims=True)
        expo = jnp.exp(score - top)
        total = jnp.sum(expo, axis=0, keepdims=True)
        prob = expo * (1.0 / total)
        both = prob * dprob
        delta = jnp.sum(both, axis=0, keepdims=True)
        return qh, dah, prob.astype(BF16), (both - prob * delta).astype(BF16)

    def close(tile, first_half, second_half):
        rows = slice(tile * QT, (tile + 1) * QT)
        span = slice(tile * QT, tile * QT + KT)
        q0, da0, p0, s0 = first_half
        q1, da1, p1, s1 = second_half
        joined = lambda x, y, axis: jnp.concatenate([x, y], axis=axis)
        dv = dot(joined(p0, p1, 1), joined(da0, da1, 0), 1, 0)
        ds = joined(s0, s1, 1)
        dk = dot(ds, joined(q0, q1, 0), 1, 0)
        dq = dot(kx_ref[span, :], ds, 0, 0)
        dq = jnp.where(rowlane < HD, dq[:, :QT], dq[:, QT:])
        dq_ref[rows, :] = jnp.transpose(dq * scale).astype(BF16)
        if tile == 0:
            dk_ref[span, :] = dk
            dv_ref[span, :] = dv
        else:
            seen = slice(tile * QT, (tile - 1) * QT + KT)
            fresh = slice((tile - 1) * QT + KT, tile * QT + KT)
            both = KT - QT
            dk_ref[seen, :] += dk[:both]
            dv_ref[seen, :] += dv[:both]
            dk_ref[fresh, :] = dk[both:]
            dv_ref[fresh, :] = dv[both:]

    opened = open_step(steps[0])
    soft = []
    for n, (tile, half) in enumerate(steps):
        later = open_step(steps[n + 1]) if n + 1 < len(steps) else None
        soft.append(soften(opened))
        opened = later
        if half == 1:
            close(tile, soft[-2], soft[-1])
    pass
    back_ref[0] = dk_ref[:WINDOW].astype(BF16)
    back_ref[1] = dv_ref[:WINDOW].astype(BF16)
    dko_ref[...] = dk_ref[WINDOW:]
    dvo_ref[...] = dv_ref[WINDOW:]


def attention_grads(first, doc_lengths, queries, halo, keys, values, grad_attn, at):
    count = queries.shape[0]
    width = halo.shape[2]
    pairs = width // LANES
    ext = count + WINDOW
    tiles = count // QT
    column = pl.BlockSpec((count, LANES), lambda i: (0, i + at))
    fresh = pl.BlockSpec((count, LANES), lambda i: (0, i))
    docs = doc_lengths.shape[0]
    return pl.pallas_call(
        attention_kernel,
        grid=(pairs,),
        in_specs=[
            pl.BlockSpec(memory_space=pltpu.SMEM),
            pl.BlockSpec((1, docs), lambda i: (0, 0)),
            column,
            pl.BlockSpec((1, WINDOW, LANES), lambda i: (0, 0, i)),
            column,
            pl.BlockSpec((1, WINDOW, LANES), lambda i: (1, 0, i)),
            column,
            column,
        ],
        out_specs=[fresh, pl.BlockSpec((2, WINDOW, LANES), lambda i: (0, 0, i)), fresh, fresh],
        out_shape=[
            jax.ShapeDtypeStruct((count, width), BF16),
            jax.ShapeDtypeStruct((2, WINDOW, width), BF16),
            jax.ShapeDtypeStruct((count, width), F32),
            jax.ShapeDtypeStruct((count, width), F32),
        ],
        scratch_shapes=[
            pltpu.VMEM((tiles, KT, QT), F32),
            pltpu.VMEM((ext, LANES), BF16),
            pltpu.VMEM((ext, LANES), BF16),
            pltpu.VMEM((ext, LANES), F32),
            pltpu.VMEM((ext, LANES), F32),
        ],
        compiler_params=params(56),
        cost_estimate=pl.CostEstimate(
            flops=10 * count * KT * width, bytes_accessed=20 * count * width,
            transcendentals=count * KT * width // HD,
        ),
        name="attention",
    )(first, doc_lengths.reshape(1, docs), queries, halo, keys, halo, values, grad_attn)


PACK = 32
SPREAD = 16


def finish_kernel(*refs):
    groups = len(GROUPS)
    parts = [refs[3 * g : 3 * g + 3] for g in range(groups)]
    (
        norm_in, wk_in, wv_in, hidden_in, out_in, gain_ref, slot_ref, mark_ref, gh_out, sent_out,
        norm_ref, dk_ref, dv_ref, back_ref, wk_ref, wv_ref, hidden_ref, out_ref,
        gh_ref, sent_ref, sems,
    ) = refs[3 * groups :]
    count, width = hidden_ref.shape
    devices = sent_ref.shape[0]
    started = []

    def bring(*pairs):
        copies = []
        for source, target in pairs:
            copies.append(pltpu.make_async_copy(source, target, sems.at[len(started)]))
            started.append(copies[-1])
            copies[-1].start()
        return copies

    def arrive(copies):
        for copy in copies:
            copy.wait()

    spans = []
    at = 0
    for pairs in GROUPS:
        spans.append(slice(at * LANES, (at + pairs) * LANES))
        at += pairs
    need_hidden = bring((hidden_in, hidden_ref))
    need_k = bring(
        *[(p[0].at[0], back_ref.at[0, :, c]) for p, c in zip(parts, spans)],
        *[(p[1], dk_ref.at[:, c]) for p, c in zip(parts, spans)],
        (wk_in, wk_ref),
    )
    need_norm = bring((norm_in, norm_ref))
    need_v = bring(
        *[(p[0].at[1], back_ref.at[1, :, c]) for p, c in zip(parts, spans)],
        *[(p[2], dv_ref.at[:, c]) for p, c in zip(parts, spans)],
        (wv_in, wv_ref),
    )
    need_out = bring((out_in, out_ref))

    def hits(place, at):
        hit = place == slot_ref[at : at + 1, :]
        for table in range(1, NG):
            hit = hit | (place == slot_ref[at + table : at + table + 1, :])
        return jnp.where(hit, 1.0, 0.0).astype(BF16)

    blocks = width // LANES
    both = NG * MAIN
    tail = CHUNK - blocks * both
    lasts = blocks * NG
    shape = (SPREAD * tail, (lasts + 2) * SPREAD)
    row = iota((shape[0], 1), 0)
    inner = lax.rem(row, tail)
    owner = row // tail
    source = jnp.where(
        inner < lasts,
        (inner // NG) * (SPREAD * NG) + owner * NG + lax.rem(inner, NG),
        inner * SPREAD + owner,
    )
    lay = jnp.where((inner < lasts + 2) & (source == iota(shape, 1)), 1.0, 0.0).astype(BF16)

    arrive(need_hidden)
    full = hidden_ref[...].astype(F32)
    inverse = lax.rsqrt(jnp.mean(full * full, axis=1, keepdims=True) + EPS)
    arrive(need_k)
    norm = dot((dk_ref[...] + back_ref[0].astype(F32)).astype(BF16), wk_ref[...], 1, 1)
    arrive(need_norm)
    norm = norm_ref[...] + norm
    arrive(need_v)
    norm = norm + dot((dv_ref[...] + back_ref[1].astype(F32)).astype(BF16), wv_ref[...], 1, 1)
    arrive(need_out)
    unit = hidden_ref[...].astype(F32) * inverse
    scaled = norm * gain_ref[...]
    through = inverse * (scaled - unit * jnp.mean(scaled * unit, axis=1, keepdims=True))
    grad_hidden = (out_ref[...].astype(F32) + through).astype(BF16)
    gh_ref[...] = grad_hidden
    leaving = bring((gh_ref, gh_out))

    cut = lambda value, c: value[:, c * LANES : (c + 1) * LANES]
    rest = dot(hits(iota((devices * NG, count), 0), NG), grad_hidden, 1, 0).astype(BF16)
    for at in range(0, devices, PACK):
        place = at * both + iota((PACK * both, count), 0)
        main = dot(hits(place, 0), grad_hidden, 1, 0)
        for c in range(0, blocks, 2):
            pair = [cut(main, c + i).reshape(PACK, both, LANES) for i in range(2)]
            sent_ref[at : at + PACK, c * both : (c + 2) * both, :] = jnp.concatenate(
                pair, axis=1
            ).astype(BF16)
        for low in range(at, at + PACK, SPREAD):
            some = rest[low * NG : (low + SPREAD) * NG]
            some = jnp.concatenate(
                [cut(some, c) for c in range(blocks)]
                + [mark_ref[part, low : low + SPREAD, :] for part in range(2)],
                axis=0,
            )
            sent_ref[low : low + SPREAD, blocks * both :, :] = (
                dot(lay, some, 1, 0).reshape(SPREAD, tail, LANES).astype(BF16)
            )
        leaving += bring((sent_ref.at[at : at + PACK], sent_out.at[at : at + PACK]))
    arrive(leaving)


def finish(parts, norm, wk, wv, hidden, gain, grad_out, slot, mark):
    count, width = hidden.shape
    devices = mark.shape[1]
    groups = len(GROUPS)
    place = pl.BlockSpec(memory_space=pl.ANY)
    small = pl.BlockSpec(memory_space=pltpu.VMEM)
    copies = 4 * groups + 6 + devices // PACK
    return pl.pallas_call(
        finish_kernel,
        in_specs=[place] * (3 * groups + 5) + [small] * 3,
        out_specs=(place, place),
        out_shape=(
            jax.ShapeDtypeStruct((count, width), BF16),
            jax.ShapeDtypeStruct((devices, CHUNK, LANES), BF16),
        ),
        scratch_shapes=[
            pltpu.VMEM((count, width), F32),
            pltpu.VMEM((count, width), F32),
            pltpu.VMEM((count, width), F32),
            pltpu.VMEM((2, WINDOW, width), BF16),
            pltpu.VMEM((width, width), BF16),
            pltpu.VMEM((width, width), BF16),
            pltpu.VMEM((count, width), BF16),
            pltpu.VMEM((count, width), BF16),
            pltpu.VMEM((count, width), BF16),
            pltpu.VMEM((devices, CHUNK, LANES), BF16),
            pltpu.SemaphoreType.DMA((copies,)),
        ],
        compiler_params=params(56),
        name="finish",
    )(
        *[array for part in parts for array in part],
        norm, wk, wv, hidden, grad_out, gain.reshape(1, width), slot, mark,
    )


COLLECT = 1024
APART = 16


def collect_kernel(got_ref, out_ref, rows_ref, mark_ref, label_ref):
    devices = got_ref.shape[0]
    blocks = rows_ref.shape[2] // LANES
    both = NG * MAIN
    tail = CHUNK - blocks * both
    mains = devices * MAIN

    table = pl.program_id(0)
    opening = (table == 0) & (pl.program_id(1) == 0)
    place = pl.program_id(1) * COLLECT + iota((COLLECT, label_ref.shape[2]), 0)

    @pl.when(opening)
    def _():
        lasts = NG * blocks
        shape = ((lasts + 2) * APART, APART * tail)
        row = iota((shape[0], 1), 0)
        device = lax.rem(row, APART)
        block = lax.rem(row // APART, blocks)
        which = row // (APART * blocks)
        source = device * tail + jnp.where(which < NG, block * NG + which, row // APART)
        pick = jnp.where(source == iota(shape, 1), 1.0, 0.0).astype(BF16)
        for at in range(0, devices, APART):
            rest = got_ref[at : at + APART, blocks * both :, :].reshape(APART * tail, LANES)
            rest = dot(pick, rest, 1, 0).astype(BF16)
            for t in range(NG):
                for c in range(blocks):
                    start = (t * blocks + c) * APART
                    rows_ref[t, mains + at : mains + at + APART, c * LANES : (c + 1) * LANES] = rest[
                        start : start + APART
                    ]
            for part in range(2):
                start = (lasts + part) * APART
                mark_ref[part, at : at + APART, :] = rest[start : start + APART]
        number = label_ref.shape[2]
        k = iota((1, number), 1)
        for t in range(NG):
            source = k // MAIN
            if t == 1:
                source = source + 1 - 2 * lax.rem(source, 2)
            source = jnp.where(k < mains, source, k - mains)
            slot = t * SLOTS + jnp.where(k < mains, lax.rem(k, MAIN), MAIN)
            take = jnp.where(slot == iota((LANES, number), 0), 1.0, 0.0).astype(BF16)
            value = MARK * dot(mark_ref[0], take, 1, 0) + dot(mark_ref[1], take, 1, 0)
            value = jnp.where(source == iota((devices, number), 0), value, 0.0)
            label_ref[t] = jnp.sum(value, axis=0, keepdims=True).astype(I32) - 1
        hit = jnp.where(place == label_ref[0], 1.0, 0.0).astype(BF16)
        low = iota((devices // 2, both, LANES), 1) < MAIN
        for c in range(0, blocks, 2):
            wide = got_ref[:, c * both : (c + 2) * both, :].astype(F32)
            for i in range(2):
                cols = slice((c + i) * LANES, (c + i + 1) * LANES)
                piece = wide[:, i * both : (i + 1) * both, :]
                piece = piece.reshape(devices // 2, 2, both, LANES)
                even, odd = piece[:, 0], piece[:, 1]
                zero = jnp.where(low, even, odd).reshape(mains, LANES)
                one = jnp.where(low, odd, even).reshape(mains, LANES)
                rows_ref[0, :mains, cols] = zero.astype(BF16)
                rows_ref[1, :mains, cols] = one.astype(BF16)
            cols = slice(c * LANES, (c + 2) * LANES)
            out_ref[0, :, cols] = dot(hit, rows_ref[0, :, cols], 1, 0).astype(BF16)

    @pl.when(jnp.logical_not(opening))
    def _():
        hit = jnp.where(place == label_ref[table], 1.0, 0.0).astype(BF16)
        out_ref[0] = dot(hit, rows_ref[table], 1, 0).astype(BF16)


def collect(got, width):
    devices = got.shape[0]
    number = devices * SLOTS
    return pl.pallas_call(
        collect_kernel,
        grid=(NG, ROWS_DEV // COLLECT),
        in_specs=[pl.BlockSpec(got.shape, lambda t, i: (0, 0, 0))],
        out_specs=pl.BlockSpec((1, COLLECT, width), lambda t, i: (t, i, 0)),
        out_shape=jax.ShapeDtypeStruct((NG, ROWS_DEV, width), BF16),
        scratch_shapes=[
            pltpu.VMEM((NG, number, width), BF16),
            pltpu.VMEM((2, devices, LANES), BF16),
            pltpu.VMEM((NG, 1, number), I32),
        ],
        compiler_params=params(28),
        name="collect",
    )(got)


def exchanged(part):
    return lax.all_to_all(part, AXES, split_axis=0, concat_axis=0, tiled=True)


def shards(
    hidden,
    gain,
    queries,
    keys,
    values,
    w_query,
    w_key,
    w_value,
    w_out,
    grad_out,
    doc_lengths,
    hash_ids,
):
    count, width = hidden.shape
    devices = lax.axis_size(AXES)
    first = (lax.axis_index(AXES) * count).astype(I32).reshape(1)
    halos = []
    at = 0
    for pairs in GROUPS:
        cols = slice(at * LANES, (at + pairs) * LANES)
        halos.append(shifted(jnp.stack([keys[:, cols], values[:, cols]]), 1))
        at += pairs
    grad_attn = dot(grad_out, w_out, 1, 1).astype(BF16)
    slot, mark = make_slots(first, hash_ids, devices)
    grad_attn, slot, mark = lax.optimization_barrier((grad_attn, slot, mark))
    parts = []
    queries_part = []
    at = 0
    for pairs, halo in zip(GROUPS, halos):
        dq, back, dk, dv = attention_grads(
            first, doc_lengths, queries, halo, keys, values, grad_attn, at
        )
        queries_part.append(dq)
        parts.append((shifted(back, -1), dk, dv))
        at += pairs
    grad_q = jnp.concatenate(lax.optimization_barrier(queries_part), axis=1)
    norm = dot(grad_q, w_query, 1, 1)
    grad_hidden, sent = finish(
        parts, norm, w_key, w_value, hidden, gain, grad_out, slot, mark
    )
    return grad_hidden, collect(exchanged(sent), width)


def solution(mesh):
    spread = P(AXES, None)
    return jax.shard_map(
        shards,
        mesh=mesh,
        in_specs=(
            spread, P(), spread, spread, spread, P(), P(), P(), P(), spread, P(), P(None, AXES),
        ),
        out_specs=(spread, P(None, AXES, None)),
        check_vma=False,
    )
```
